32 devices in a mesh: dap: 16 (over z, y, core), heads: 2 (over x).
Axes of the slice: x: 2, y: 2, z: 4, core: 2. Of those that a mesh axis runs over, the one named last changes fastest.
Arguments:
- pair: bfloat16 [96, 96, 128], P('dap'), may hold values from -6 to 6
- ln_gain: float32 [128], replicated, may hold values from 0.1 to 1.9
- ln_shift: float32 [128], replicated, may hold values from -3 to 3
- w_project: bfloat16 [128, 4, 128], P(None, None, 'heads'), may hold values from -0.5 to 0.5
- w_bias: bfloat16 [128, 4], P(None, 'heads'), may hold values from -2 to 2
- w_out: bfloat16 [128, 128], P('heads'), may hold values from -0.5 to 0.5
Outputs:
- update: bfloat16 [96, 96, 128], P(('dap', 'heads'))
The draws below stay inside these ranges and needn't reach their ends.
All inputs are finite; a program needn't handle non-finite values.
Results may differ from the reference program's by a relative error of at most 0.0039.
The reference program's roundings to bfloat16 on the way (of `normed`, `queries`, `gating`, `weights` and `gated_out`) count: a program that leaves them out, or rounds other values in their place, can miss the bound.
Values may be sent and summed in bfloat16 or wider, within the bound.
A program may use at most 64 MiB of HBM per device.

```python
import math
import jax
import jax.numpy as jnp
from jax import lax

C = 128
H = 4
DH = 32
N = 96


def draw_w_bias(key, part):
    key = jax.random.fold_in(key, 11)
    values = jnp.clip(jax.random.normal(key, (C, H), jnp.float32), -4.0, 4.0) * 0.0625
    return values.astype(jnp.bfloat16)


def steps_of(stream_key, extent, shards, low, largest):
    def one(dim, blocks):
        heights = jax.random.uniform(jax.random.fold_in(jax.random.fold_in(stream_key, 6), dim), (blocks,), jnp.float32, low / len(shards), largest / len(shards))
        return jnp.repeat(jnp.exp(heights), extent[dim] // blocks).reshape((-1,) + (1,) * (len(extent) - dim - 1))

    gain = one(*shards[0])
    for cut in shards[1:]:
        gain = gain * one(*cut)
    return gain


def scatter_about(stream_key, shape, width, reach, pieces=(), held_as=jnp.bfloat16):
    loudness = steps_of(stream_key, shape, pieces, -0.22, 0.18) if pieces else 1.0
    entries = jax.random.normal(stream_key, shape, jnp.float32) * width * loudness
    return jnp.minimum(jnp.maximum(entries, -reach), reach).astype(held_as)


def setup_inputs(seed: int = 0) -> dict:
    seeds = jax.random.split(jax.random.key(seed), 7)
    return {
        "pair": scatter_about(seeds[0], (N, N, C), 1.0, 6.0, ((0, 16),)),
        "ln_gain": jnp.clip(1.0 + 0.18 * jax.random.normal(seeds[1], (C,), jnp.float32), 0.1, 1.9),
        "ln_shift": scatter_about(seeds[2], (C,), 0.5, 3.0, (), jnp.float32),
        "w_project": scatter_about(seeds[3], (C, 4, H * DH), C ** -0.5, 0.5, ((2, 2),)),
        "w_bias": draw_w_bias(jax.random.fold_in(seeds[6], 71), 0),
        "w_out": scatter_about(seeds[5], (H * DH, C), (H * DH) ** -0.5, 0.5, ((0, 2),)),
    }


def normalize(pair, ln_gain, ln_shift):
    values_f = pair.astype(jnp.float32)
    average = lax.optimization_barrier(jnp.mean(values_f, axis=-1, keepdims=True))
    centred = values_f - average
    variance = lax.optimization_barrier(jnp.mean(centred * centred, axis=-1, keepdims=True))
    return (centred * lax.rsqrt(variance + 1e-05) * ln_gain + ln_shift).astype(jnp.bfloat16)

def project_entries(normed, flat_w):
    projected = jnp.dot(normed, flat_w, preferred_element_type=jnp.float32)
    head_width = flat_w.shape[1] // 4
    head_part = projected[..., :3 * head_width].astype(jnp.bfloat16)
    gating = jax.nn.sigmoid(projected[..., 3 * head_width:]).astype(jnp.bfloat16)
    return jnp.concatenate([head_part, gating], axis=-1)

def reference(pair, ln_gain, ln_shift, w_project, w_bias, w_out):
    normed = normalize(pair, ln_gain, ln_shift)
    pair_bias = jnp.einsum('abc,ch->hab', normed.astype(jnp.float32), w_bias.astype(jnp.float32))
    bias_key_last = jnp.swapaxes(pair_bias, 1, 2)
    flat_w = w_project.reshape(C, 4 * H * DH)
    col_block = 8

    def one_block(first_col):
        columns = lax.dynamic_slice_in_dim(normed, first_col, col_block, 1)
        packed = project_entries(columns, flat_w).reshape(N, col_block, 4, H, DH)
        queries = packed[:, :, 0].astype(jnp.float32)
        keys_all = packed[:, :, 1].astype(jnp.float32)
        values = packed[:, :, 2].astype(jnp.float32)
        gating = packed[:, :, 3].astype(jnp.float32)
        scores = jnp.einsum('ibhc,kbhc->bhik', queries, keys_all) * (1.0 / math.sqrt(DH)) + bias_key_last[None]
        highest = lax.optimization_barrier(jnp.max(scores, axis=-1, keepdims=True))
        exponent = jnp.exp(scores - highest)
        totals = lax.optimization_barrier(jnp.sum(exponent, axis=-1))
        weights = exponent.astype(jnp.bfloat16)
        attended = jnp.einsum('bhik,kbhc->ibhc', weights.astype(jnp.float32), values)
        attended = attended / jnp.transpose(totals, (2, 0, 1))[..., None]
        gated_out = (attended * gating).astype(jnp.bfloat16).reshape(N * col_block, H * DH)
        return jnp.dot(gated_out, w_out, preferred_element_type=jnp.float32).astype(jnp.bfloat16).reshape(N, col_block, C)
    starts = jnp.arange(0, N, col_block, dtype=jnp.int32)
    stacked = lax.map(one_block, starts)
    return jnp.transpose(stacked, (1, 0, 2, 3)).reshape(N, N, C)
```

```python
import functools
import math

import jax
import jax.numpy as jnp
from jax import lax
from jax.experimental import pallas as pl
from jax.experimental.pallas import tpu as pltpu
from jax.sharding import PartitionSpec as P

MESH = pl.DeviceIdType.MESH
F32 = jnp.float32
BF16 = jnp.bfloat16
NT = (((1,), (1,)), ((), ()))
VMEM_BYTES = 60 * 1024 * 1024


def up(size, unit):
    return -(-size // unit) * unit


def nt_dot(left, right):
    return lax.dot_general(left, right, NT, preferred_element_type=F32)


def kernel(
    dims,
    pair_hbm,
    gain_hbm,
    shift_hbm,
    bias_hbm,
    project_hbm,
    w_out_hbm,
    out_ref,
    pair_ref,
    gain_ref,
    shift_ref,
    bias_ref,
    normed,
    stage,
    x_send,
    x_recv,
    tokens,
    w_all,
    b_pad,
    b_recv,
    bias,
    gated,
    g_stage,
    g_send,
    g_recv,
    projected,
    load_sem,
    w_send_sem,
    w_recv_sem,
    x_send_sem,
    x_recv_sem,
    b_send_sem,
    b_recv_sem,
    g_send_sem,
    g_recv_sem,
):
    n, groups, rows, width, cols, heads, size = dims
    own_heads = heads // groups
    inner = own_heads * size
    devices = n * groups
    own_rows = rows // groups
    d = lax.axis_index("dap")
    g = lax.axis_index("heads")
    me = g * n + d
    quad = min(4, n)
    slabs = n // quad
    z, r = d // quad, lax.rem(d, quad)
    planes = [g, 1 - g]
    dap_at = [lax.rem(d + offset, n) for offset in range(n)]
    slab_at = [lax.rem(z + back, slabs) * quad for back in range(slabs)]
    near_at = [lax.rem(r + near, quad) for near in range(quad)]

    barrier = pltpu.get_barrier_semaphore()
    others = [(k % n, k // n) for k in range(1, devices)]
    for offset, plane in others:
        pl.semaphore_signal(
            barrier, inc=1, device_id=(dap_at[offset], planes[plane]), device_id_type=MESH
        )

    low_out = 4 * inner
    loads = [
        pltpu.make_async_copy(pair_hbm, pair_ref, load_sem.at[0]),
        pltpu.make_async_copy(gain_hbm, gain_ref, load_sem.at[4]),
        pltpu.make_async_copy(shift_hbm, shift_ref, load_sem.at[5]),
    ]
    w_loads = [
        pltpu.make_async_copy(bias_hbm, bias_ref, load_sem.at[1]),
        pltpu.make_async_copy(project_hbm, w_all.at[g, pl.ds(0, low_out)], load_sem.at[2]),
        pltpu.make_async_copy(w_out_hbm, w_all.at[g, pl.ds(low_out, inner)], load_sem.at[3]),
    ]
    for copy in loads + w_loads:
        copy.start()

    for copy in loads:
        copy.wait()
    gain = gain_ref[...]
    shift = shift_ref[...]
    for a in range(rows):
        values = pair_ref[a].astype(F32)
        average = jnp.mean(values, axis=-1, keepdims=True)
        centred = values - average
        variance = jnp.mean(centred * centred, axis=-1, keepdims=True)
        normed[a * width : (a + 1) * width, :] = (
            centred * lax.rsqrt(variance + 1e-05) * gain + shift
        )

    x_rows = x_send.shape[1]
    for a in range(rows):
        for c in range(cols):
            start = pl.multiple_of(a * width + c * devices + g * n, 8)
            stage[pl.ds(a * cols + c, n, x_rows), :] = normed[pl.ds(start, n), :]
    x_send[...] = stage[...].reshape(n, x_rows, -1).astype(BF16)

    w_loads[0].wait()
    b_pad[0:own_heads, :] = bias_ref[...]
    w_bias = b_pad[...]
    for a in range(rows):
        part = nt_dot(w_bias, normed[a * width : (a + 1) * width, :].astype(BF16))
        for h in range(own_heads):
            row = h * rows + a
            b_recv[d, g, row : row + 1, 0:width] = part[h : h + 1]
    for copy in w_loads[1:]:
        copy.wait()

    pl.semaphore_wait(barrier, devices - 1)

    def send(src, dst, send_sem, recv_sem, other, plane=g):
        copy = pltpu.make_async_remote_copy(
            src_ref=src,
            dst_ref=dst,
            send_sem=send_sem,
            recv_sem=recv_sem,
            device_id=(other, plane),
            device_id_type=MESH,
        )
        copy.start()
        return copy

    def drain(ref, sem):
        pltpu.make_async_copy(ref, ref, sem).wait()

    b_used = own_heads * rows
    own_bias = b_recv.at[d, g, pl.ds(0, b_used)]
    first = [(back, plane) for plane in range(groups) for back in range(slabs)][1:]
    across = {}
    for back, plane in first:
        k = back * groups + plane
        across[back, plane] = send(
            own_bias, own_bias, b_send_sem.at[0], b_recv_sem.at[k], slab_at[back] + r, planes[plane]
        )

    far = [near + back * quad for back in range(1, slabs) for near in range(quad)]
    for offset in far + list(range(1, quad)):
        other = slab_at[offset // quad] + near_at[offset % quad]
        send(x_send.at[other], x_recv.at[d], x_send_sem, x_recv_sem, other)
    own_w = w_all.at[g]
    w_copy = send(own_w, own_w, w_send_sem, w_recv_sem, d, planes[1])
    x_recv[d] = x_send[d]

    for back in range(slabs):
        for plane in range(groups):
            if back or plane:
                across[back, plane].wait_recv()
        block = slab_at[(slabs - back) % slabs] + r
        both = b_recv.at[block, :, pl.ds(0, b_used)]
        for near in range(1, quad):
            send(both, both, b_send_sem.at[1], b_recv_sem.at[0], slab_at[0] + near_at[near])

    drain(x_recv.at[pl.ds(0, n - 1)], x_recv_sem)
    stage[...] = x_recv[...].reshape(n * x_rows, -1).astype(F32)
    for a in range(rows):
        for c in range(cols):
            tokens[pl.ds(c * width + a, n, rows), :] = stage[pl.ds(a * cols + c, n, x_rows), :]
    entries = tokens[...].astype(BF16)

    w_copy.wait_recv()

    def weight(t):
        low = t * inner
        return jnp.concatenate([w_all[k, low : low + inner, :] for k in range(groups)], axis=0)

    queries = nt_dot(entries, weight(0)).astype(BF16)
    keys = nt_dot(entries, weight(1)).astype(BF16)
    w_value, w_gate = weight(2), weight(3)
    lane = lax.broadcasted_iota(jnp.int32, (width, heads * size), 1) // size
    scores, values, gating = [], [], []
    for c in range(cols):
        part = slice(c * width, (c + 1) * width)
        key = keys[part]
        stacked = jnp.concatenate(
            [jnp.where(lane == h, key, jnp.zeros_like(key)) for h in range(heads)], axis=0
        )
        scores.append(nt_dot(stacked, queries[part]))
        values.append(nt_dot(w_value, entries[part]).astype(BF16))
        gating.append(jax.nn.sigmoid(nt_dot(w_gate, entries[part])).astype(BF16).astype(F32))

    passed = slabs * (quad - 1)
    drain(b_recv.at[pl.ds(0, passed), :, pl.ds(0, b_used)], b_recv_sem.at[0])
    b_rows = b_recv.shape[2]
    gathered = b_recv.reshape(n * groups * b_rows, 128)
    for h in range(heads):
        for a in range(rows):
            first_row = h // own_heads * b_rows + h % own_heads * rows + a
            bias[pl.ds(h * width + a, n, rows), :] = gathered[
                pl.ds(first_row, n, groups * b_rows), :
            ]

    scale = 1.0 / math.sqrt(size)
    for c in range(cols):
        parts = []
        for h in range(heads):
            part = slice(h * width, (h + 1) * width)
            score = scores[c][part] * scale + bias[part, 0:width]
            exponent = jnp.exp(score - jnp.max(score, axis=0, keepdims=True))
            total = jnp.sum(exponent, axis=0, keepdims=True)
            head = slice(h * size, (h + 1) * size)
            attended = jnp.dot(values[c][head], exponent.astype(BF16), preferred_element_type=F32)
            parts.append(attended / total * gating[c][head])
        gated[c * width : (c + 1) * width, :] = jnp.concatenate(parts, axis=0).T

    g_rows = g_send.shape[1]
    for i in range(own_rows):
        for c in range(cols):
            g_stage[pl.ds(i * cols + c, devices, g_rows), :] = gated[
                pl.ds(c * width + i, devices, own_rows), :
            ]
    g_send[...] = g_stage[...].reshape(devices, g_rows, -1).astype(BF16)

    for offset, plane in sorted(others, key=lambda o: -min(o[0], n - o[0])):
        other_d, other_g = dap_at[offset], planes[plane]
        send(
            g_send.at[other_d * groups + other_g],
            g_recv.at[me],
            g_send_sem,
            g_recv_sem,
            other_d,
            other_g,
        )
    g_recv[me] = g_send[d * groups + g]
    drain(b_recv.at[pl.ds(0, len(first)), 0, pl.ds(0, b_used)], b_send_sem.at[0])
    drain(b_recv.at[pl.ds(0, passed), :, pl.ds(0, b_used)], b_send_sem.at[1])
    drain(x_send.at[pl.ds(0, n - 1)], x_send_sem)
    w_copy.wait_send()
    drain(g_send.at[pl.ds(0, devices - 1)], g_send_sem)
    w_out = jnp.concatenate([w_all[k, low_out : low_out + inner, :] for k in range(groups)], axis=0)
    drain(g_recv.at[pl.ds(0, devices - 1)], g_recv_sem)
    projected[...] = jnp.dot(
        g_recv[...].reshape(devices * g_rows, -1), w_out, preferred_element_type=F32
    )
    for i in range(own_rows):
        for c in range(cols):
            out_ref[i, c * devices : (c + 1) * devices, :] = projected[
                pl.ds(i * cols + c, devices, g_rows), :
            ].astype(BF16)


def fused(n, groups, pair, ln_gain, ln_shift, w_project, w_bias, w_out):
    rows, width, channels = pair.shape
    own_heads = w_bias.shape[1]
    heads = own_heads * groups
    size = w_project.shape[2] // own_heads
    devices = n * groups
    cols = width // devices
    own_rows = rows // groups
    inner = own_heads * size
    w_rows = 5 * inner
    b_rows = up(own_heads * rows, 8)
    x_rows = up(rows * cols, 16)
    g_rows = up(own_rows * cols, 16)
    dims = (n, groups, rows, width, cols, heads, size)
    vmem = pl.BlockSpec(memory_space=pltpu.VMEM)
    hbm = pl.BlockSpec(memory_space=pl.ANY)
    sems = pltpu.SemaphoreType.DMA
    return pl.pallas_call(
        functools.partial(kernel, dims),
        out_shape=pltpu.VMEM((own_rows, width, channels), BF16),
        in_specs=[hbm] * 6,
        out_specs=vmem,
        scratch_shapes=[
            pltpu.VMEM((rows, width, channels), BF16),
            pltpu.VMEM((1, channels), F32),
            pltpu.VMEM((1, channels), F32),
            pltpu.VMEM((own_heads, channels), BF16),
            pltpu.VMEM((rows * width, channels), F32),
            pltpu.VMEM((n * x_rows, channels), F32),
            pltpu.VMEM((n, x_rows, channels), BF16),
            pltpu.VMEM((n, x_rows, channels), BF16),
            pltpu.VMEM((cols * width, channels), F32),
            pltpu.VMEM((groups, w_rows, channels), BF16),
            pltpu.VMEM((16, channels), BF16),
            pltpu.VMEM((n, groups, b_rows, 128), F32),
            pltpu.VMEM((heads * width, 128), F32),
            pltpu.VMEM((cols * width, heads * size), F32),
            pltpu.VMEM((devices * g_rows, heads * size), F32),
            pltpu.VMEM((devices, g_rows, heads * size), BF16),
            pltpu.VMEM((devices, g_rows, heads * size), BF16),
            pltpu.VMEM((devices * g_rows, channels), F32),
            sems((6,)),
            sems(()),
            sems(()),
            sems(()),
            sems(()),
            sems((2,)),
            sems((n // min(4, n) * groups,)),
            sems(()),
            sems(()),
        ],
        compiler_params=pltpu.CompilerParams(
            collective_id=0, has_side_effects=True, vmem_limit_bytes=VMEM_BYTES
        ),
    )(
        pair,
        ln_gain.reshape(1, -1),
        ln_shift.reshape(1, -1),
        w_bias.T,
        jnp.transpose(w_project, (1, 2, 0)).reshape(-1, channels),
        w_out,
    )


def normalize(pair, ln_gain, ln_shift):
    values_f = pair.astype(jnp.float32)
    average = jnp.mean(values_f, axis=-1, keepdims=True)
    centred = values_f - average
    variance = jnp.mean(centred * centred, axis=-1, keepdims=True)
    return (centred * lax.rsqrt(variance + 1e-05) * ln_gain + ln_shift).astype(jnp.bfloat16)


def project_entries(normed, flat_w):
    projected = jnp.dot(normed, flat_w, preferred_element_type=jnp.float32)
    head_width = flat_w.shape[1] // 4
    head_part = projected[..., : 3 * head_width].astype(jnp.bfloat16)
    gating = jax.nn.sigmoid(projected[..., 3 * head_width :]).astype(jnp.bfloat16)
    return jnp.concatenate([head_part, gating], axis=-1)


def local(pair, ln_gain, ln_shift, w_project, w_bias, w_out):
    row_count, width_n, channels = pair.shape
    heads_here = w_bias.shape[1]
    head_size = w_project.shape[2] // heads_here
    flat_w = w_project.reshape(channels, -1)
    normed_rows = normalize(pair, ln_gain, ln_shift)
    bias_rows = jnp.einsum("abc,ch->hab", normed_rows, w_bias, preferred_element_type=jnp.float32)
    bias_all = lax.all_gather(bias_rows, "dap", axis=1, tiled=True)
    bias_key_last = jnp.swapaxes(bias_all, 1, 2)
    dap_count = lax.axis_size("dap")
    blocks = pair.reshape(row_count, dap_count, width_n // dap_count, channels)
    packed = project_entries(
        normalize(
            lax.all_to_all(blocks, "dap", split_axis=1, concat_axis=0, tiled=True),
            ln_gain,
            ln_shift,
        ),
        flat_w,
    )
    packed = packed.reshape(width_n, row_count, -1)

    def attend(index):
        column_data = lax.dynamic_index_in_dim(packed, index, 1, keepdims=False)
        pieces = column_data.reshape(width_n, 4, heads_here, head_size)
        scores = jnp.einsum(
            "ihc,khc->hik", pieces[:, 0], pieces[:, 1], preferred_element_type=jnp.float32
        )
        scores = scores * (1.0 / math.sqrt(head_size)) + bias_key_last
        highest = jnp.max(scores, axis=-1, keepdims=True)
        exponent = jnp.exp(scores - highest)
        totals = jnp.sum(exponent, axis=-1)
        weights = exponent.astype(jnp.bfloat16)
        attended = jnp.einsum(
            "hik,khc->ihc", weights, pieces[:, 2], preferred_element_type=jnp.float32
        )
        attended = attended / jnp.swapaxes(totals, 0, 1)[..., None]
        gated_out = (attended * pieces[:, 3].astype(jnp.float32)).astype(jnp.bfloat16)
        return gated_out.reshape(width_n, heads_here * head_size)

    gated_cols = lax.map(attend, jnp.arange(row_count, dtype=jnp.int32))
    returned = lax.all_to_all(
        gated_cols.reshape(row_count, -1), "dap", split_axis=1, concat_axis=0, tiled=True
    )
    returned = returned.reshape(width_n, row_count, heads_here * head_size)
    update = lax.psum_scatter(
        jnp.einsum("jic,cd->ijd", returned, w_out, preferred_element_type=jnp.float32),
        "heads",
        scatter_dimension=0,
        tiled=True,
    )
    return update.astype(jnp.bfloat16)


def fits(mesh, pair, w_bias):
    n, groups = mesh.shape["dap"], mesh.shape["heads"]
    rows, width, channels = pair.shape
    devices = n * groups
    heads = w_bias.shape[1] * groups
    return (
        groups == 2
        and channels == 128
        and width <= 128
        and width % devices == 0
        and width % 32 == 0
        and n % 8 == 0
        and rows % groups == 0
    )


def solution(mesh):
    n, groups = mesh.shape["dap"], mesh.shape["heads"]

    def run(pair, ln_gain, ln_shift, w_project, w_bias, w_out):
        if fits(mesh, pair, w_bias):
            return fused(n, groups, pair, ln_gain, ln_shift, w_project, w_bias, w_out)
        return local(pair, ln_gain, ln_shift, w_project, w_bias, w_out)

    in_specs = (
        P("dap", None, None),
        P(),
        P(),
        P(None, None, "heads"),
        P(None, "heads"),
        P("heads", None),
    )
    out_specs = P(("dap", "heads"), None, None)
    return jax.shard_map(run, mesh=mesh, in_specs=in_specs, out_specs=out_specs, check_vma=False)
```

```python
import functools
import math

import jax
import jax.numpy as jnp
from jax import lax
from jax.experimental import pallas as pl
from jax.experimental.pallas import tpu as pltpu
from jax.sharding import PartitionSpec as P

MESH = pl.DeviceIdType.MESH
F32 = jnp.float32
BF16 = jnp.bfloat16
NT = (((1,), (1,)), ((), ()))
VMEM_BYTES = 60 * 1024 * 1024


def up(size, unit):
    return -(-size // unit) * unit


def nt_dot(left, right):
    return lax.dot_general(left, right, NT, preferred_element_type=F32)


def kernel(
    dims,
    pair_hbm,
    gain_hbm,
    shift_hbm,
    bias_hbm,
    project_hbm,
    w_out_hbm,
    out_ref,
    pair_ref,
    gain_ref,
    shift_ref,
    bias_ref,
    normed,
    stage,
    x_send,
    x_recv,
    tokens,
    w_all,
    b_pad,
    b_recv,
    bias,
    gated,
    g_stage,
    g_send,
    g_recv,
    projected,
    load_sem,
    w_send_sem,
    w_recv_sem,
    x_send_sem,
    x_recv_sem,
    b_send_sem,
    b_recv_sem,
    g_send_sem,
    g_recv_sem,
):
    n, groups, rows, width, cols, heads, size = dims
    own_heads = heads // groups
    inner = own_heads * size
    devices = n * groups
    own_rows = rows // groups
    d = lax.axis_index("dap")
    g = lax.axis_index("heads")
    me = g * n + d
    planes = [g, 1 - g]
    dap_at = [lax.rem(d + offset, n) for offset in range(n)]

    low_out = 4 * inner
    loads = [
        pltpu.make_async_copy(pair_hbm, pair_ref, load_sem.at[0]),
        pltpu.make_async_copy(gain_hbm, gain_ref, load_sem.at[4]),
        pltpu.make_async_copy(shift_hbm, shift_ref, load_sem.at[5]),
    ]
    w_loads = [
        pltpu.make_async_copy(bias_hbm, bias_ref, load_sem.at[1]),
        pltpu.make_async_copy(project_hbm, w_all.at[g, pl.ds(0, low_out)], load_sem.at[2]),
        pltpu.make_async_copy(w_out_hbm, w_all.at[g, pl.ds(low_out, inner)], load_sem.at[3]),
    ]
    for copy in loads + w_loads:
        copy.start()

    barrier = pltpu.get_barrier_semaphore()
    others = [(k % n, k // n) for k in range(1, devices)]
    for offset, plane in others:
        pl.semaphore_signal(
            barrier, inc=1, device_id=(dap_at[offset], planes[plane]), device_id_type=MESH
        )

    for copy in loads:
        copy.wait()
    gain = gain_ref[...]
    shift = shift_ref[...]
    for a in range(rows):
        values = pair_ref[a].astype(F32)
        average = jnp.mean(values, axis=-1, keepdims=True)
        centred = values - average
        variance = jnp.mean(centred * centred, axis=-1, keepdims=True)
        normed[a * width : (a + 1) * width, :] = (
            centred * lax.rsqrt(variance + 1e-05) * gain + shift
        )

    x_rows = x_send.shape[1]
    for a in range(rows):
        for c in range(cols):
            start = pl.multiple_of(a * width + c * devices + g * n, 8)
            stage[pl.ds(a * cols + c, n, x_rows), :] = normed[pl.ds(start, n), :]
    x_send[...] = stage[...].reshape(n, x_rows, -1).astype(BF16)

    w_loads[0].wait()
    b_pad[0:own_heads, :] = bias_ref[...]
    w_bias = b_pad[...]
    for a in range(rows):
        part = nt_dot(w_bias, normed[a * width : (a + 1) * width, :].astype(BF16))
        for h in range(own_heads):
            row = h * rows + a
            b_recv[d * groups + g, row : row + 1, 0:width] = part[h : h + 1]
    for copy in w_loads[1:]:
        copy.wait()

    pl.semaphore_wait(barrier, devices - 1)

    def send(src, dst, send_sem, recv_sem, other, plane=g):
        copy = pltpu.make_async_remote_copy(
            src_ref=src,
            dst_ref=dst,
            send_sem=send_sem,
            recv_sem=recv_sem,
            device_id=(other, plane),
            device_id_type=MESH,
        )
        copy.start()
        return copy

    def drain(ref, sem):
        pltpu.make_async_copy(ref, ref, sem).wait()

    def drain_bias(sem):
        drain(b_recv.at[pl.ds(0, devices - 1), pl.ds(0, b_used)], sem)

    far = sorted(others, key=lambda o: -min(o[0], n - o[0]))
    for offset, plane in far:
        if plane == 0:
            send(x_send.at[dap_at[offset]], x_recv.at[d], x_send_sem, x_recv_sem, dap_at[offset])
    b_used = own_heads * rows
    own_bias = b_recv.at[d * groups + g, pl.ds(0, b_used)]
    for offset, plane in far:
        send(own_bias, own_bias, b_send_sem, b_recv_sem, dap_at[offset], planes[plane])
    own_w = w_all.at[g]
    w_copy = send(own_w, own_w, w_send_sem, w_recv_sem, d, planes[1])
    x_recv[d] = x_send[d]

    drain(x_recv.at[pl.ds(0, n - 1)], x_recv_sem)
    stage[...] = x_recv[...].reshape(n * x_rows, -1).astype(F32)
    for a in range(rows):
        for c in range(cols):
            tokens[pl.ds(c * width + a, n, rows), :] = stage[pl.ds(a * cols + c, n, x_rows), :]
    entries = tokens[...].astype(BF16)

    w_copy.wait_recv()

    def weight(t):
        low = t * inner
        return jnp.concatenate([w_all[k, low : low + inner, :] for k in range(groups)], axis=0)

    queries = nt_dot(entries, weight(0)).astype(BF16)
    keys = nt_dot(entries, weight(1)).astype(BF16)
    w_value, w_gate = weight(2), weight(3)
    lane = lax.broadcasted_iota(jnp.int32, (width, heads * size), 1) // size
    scores, values, gating = [], [], []
    for c in range(cols):
        part = slice(c * width, (c + 1) * width)
        key = keys[part]
        stacked = jnp.concatenate(
            [jnp.where(lane == h, key, jnp.zeros_like(key)) for h in range(heads)], axis=0
        )
        scores.append(nt_dot(stacked, queries[part]))
        values.append(nt_dot(w_value, entries[part]).astype(BF16))
        gating.append(jax.nn.sigmoid(nt_dot(w_gate, entries[part])).astype(BF16).astype(F32))

    drain_bias(b_recv_sem)
    b_rows = b_recv.shape[1]
    gathered = b_recv.reshape(n * groups * b_rows, 128)
    for h in range(heads):
        for a in range(rows):
            first_row = h // own_heads * b_rows + h % own_heads * rows + a
            bias[pl.ds(h * width + a, n, rows), :] = gathered[
                pl.ds(first_row, n, groups * b_rows), :
            ]

    scale = 1.0 / math.sqrt(size)
    for c in range(cols):
        parts = []
        for h in range(heads):
            part = slice(h * width, (h + 1) * width)
            score = scores[c][part] * scale + bias[part, 0:width]
            exponent = jnp.exp(score - jnp.max(score, axis=0, keepdims=True))
            total = jnp.sum(exponent, axis=0, keepdims=True)
            head = slice(h * size, (h + 1) * size)
            attended = jnp.dot(values[c][head], exponent.astype(BF16), preferred_element_type=F32)
            parts.append(attended / total * gating[c][head])
        gated[c * width : (c + 1) * width, :] = jnp.concatenate(parts, axis=0).T

    g_rows = g_send.shape[1]
    for i in range(own_rows):
        for c in range(cols):
            g_stage[pl.ds(i * cols + c, devices, g_rows), :] = gated[
                pl.ds(c * width + i, devices, own_rows), :
            ]
    g_send[...] = g_stage[...].reshape(devices, g_rows, -1).astype(BF16)

    for offset, plane in far:
        other_d, other_g = dap_at[offset], planes[plane]
        send(
            g_send.at[other_d * groups + other_g],
            g_recv.at[me],
            g_send_sem,
            g_recv_sem,
            other_d,
            other_g,
        )
    g_recv[me] = g_send[d * groups + g]
    drain_bias(b_send_sem)
    drain(x_send.at[pl.ds(0, n - 1)], x_send_sem)
    w_copy.wait_send()
    drain(g_send.at[pl.ds(0, devices - 1)], g_send_sem)
    w_out = jnp.concatenate([w_all[k, low_out : low_out + inner, :] for k in range(groups)], axis=0)
    drain(g_recv.at[pl.ds(0, devices - 1)], g_recv_sem)
    projected[...] = jnp.dot(
        g_recv[...].reshape(devices * g_rows, -1), w_out, preferred_element_type=F32
    )
    for i in range(own_rows):
        for c in range(cols):
            out_ref[i, c * devices : (c + 1) * devices, :] = projected[
                pl.ds(i * cols + c, devices, g_rows), :
            ].astype(BF16)


def fused(n, groups, pair, ln_gain, ln_shift, w_project, w_bias, w_out):
    rows, width, channels = pair.shape
    own_heads = w_bias.shape[1]
    heads = own_heads * groups
    size = w_project.shape[2] // own_heads
    devices = n * groups
    cols = width // devices
    own_rows = rows // groups
    inner = own_heads * size
    w_rows = 5 * inner
    b_rows = up(own_heads * rows, 8)
    x_rows = up(rows * cols, 16)
    g_rows = up(own_rows * cols, 16)
    dims = (n, groups, rows, width, cols, heads, size)
    vmem = pl.BlockSpec(memory_space=pltpu.VMEM)
    hbm = pl.BlockSpec(memory_space=pl.ANY)
    sems = pltpu.SemaphoreType.DMA
    return pl.pallas_call(
        functools.partial(kernel, dims),
        out_shape=pltpu.VMEM((own_rows, width, channels), BF16),
        in_specs=[hbm] * 6,
        out_specs=vmem,
        scratch_shapes=[
            pltpu.VMEM((rows, width, channels), BF16),
            pltpu.VMEM((1, channels), F32),
            pltpu.VMEM((1, channels), F32),
            pltpu.VMEM((own_heads, channels), BF16),
            pltpu.VMEM((rows * width, channels), F32),
            pltpu.VMEM((n * x_rows, channels), F32),
            pltpu.VMEM((n, x_rows, channels), BF16),
            pltpu.VMEM((n, x_rows, channels), BF16),
            pltpu.VMEM((cols * width, channels), F32),
            pltpu.VMEM((groups, w_rows, channels), BF16),
            pltpu.VMEM((16, channels), BF16),
            pltpu.VMEM((devices, b_rows, 128), F32),
            pltpu.VMEM((heads * width, 128), F32),
            pltpu.VMEM((cols * width, heads * size), F32),
            pltpu.VMEM((devices * g_rows, heads * size), F32),
            pltpu.VMEM((devices, g_rows, heads * size), BF16),
            pltpu.VMEM((devices, g_rows, heads * size), BF16),
            pltpu.VMEM((devices * g_rows, channels), F32),
            sems((6,)),
            sems(()),
            sems(()),
            sems(()),
            sems(()),
            sems(()),
            sems(()),
            sems(()),
            sems(()),
        ],
        compiler_params=pltpu.CompilerParams(
            collective_id=0, has_side_effects=True, vmem_limit_bytes=VMEM_BYTES
        ),
    )(
        pair,
        ln_gain.reshape(1, -1),
        ln_shift.reshape(1, -1),
        w_bias.T,
        jnp.transpose(w_project, (1, 2, 0)).reshape(-1, channels),
        w_out,
    )


def normalize(pair, ln_gain, ln_shift):
    values_f = pair.astype(jnp.float32)
    average = jnp.mean(values_f, axis=-1, keepdims=True)
    centred = values_f - average
    variance = jnp.mean(centred * centred, axis=-1, keepdims=True)
    return (centred * lax.rsqrt(variance + 1e-05) * ln_gain + ln_shift).astype(jnp.bfloat16)


def project_entries(normed, flat_w):
    projected = jnp.dot(normed, flat_w, preferred_element_type=jnp.float32)
    head_width = flat_w.shape[1] // 4
    head_part = projected[..., : 3 * head_width].astype(jnp.bfloat16)
    gating = jax.nn.sigmoid(projected[..., 3 * head_width :]).astype(jnp.bfloat16)
    return jnp.concatenate([head_part, gating], axis=-1)


def local(pair, ln_gain, ln_shift, w_project, w_bias, w_out):
    row_count, width_n, channels = pair.shape
    heads_here = w_bias.shape[1]
    head_size = w_project.shape[2] // heads_here
    flat_w = w_project.reshape(channels, -1)
    normed_rows = normalize(pair, ln_gain, ln_shift)
    bias_rows = jnp.einsum("abc,ch->hab", normed_rows, w_bias, preferred_element_type=jnp.float32)
    bias_all = lax.all_gather(bias_rows, "dap", axis=1, tiled=True)
    bias_key_last = jnp.swapaxes(bias_all, 1, 2)
    dap_count = lax.axis_size("dap")
    blocks = pair.reshape(row_count, dap_count, width_n // dap_count, channels)
    packed = project_entries(
        normalize(
            lax.all_to_all(blocks, "dap", split_axis=1, concat_axis=0, tiled=True),
            ln_gain,
            ln_shift,
        ),
        flat_w,
    )
    packed = packed.reshape(width_n, row_count, -1)

    def attend(index):
        column_data = lax.dynamic_index_in_dim(packed, index, 1, keepdims=False)
        pieces = column_data.reshape(width_n, 4, heads_here, head_size)
        scores = jnp.einsum(
            "ihc,khc->hik", pieces[:, 0], pieces[:, 1], preferred_element_type=jnp.float32
        )
        scores = scores * (1.0 / math.sqrt(head_size)) + bias_key_last
        highest = jnp.max(scores, axis=-1, keepdims=True)
        exponent = jnp.exp(scores - highest)
        totals = jnp.sum(exponent, axis=-1)
        weights = exponent.astype(jnp.bfloat16)
        attended = jnp.einsum(
            "hik,khc->ihc", weights, pieces[:, 2], preferred_element_type=jnp.float32
        )
        attended = attended / jnp.swapaxes(totals, 0, 1)[..., None]
        gated_out = (attended * pieces[:, 3].astype(jnp.float32)).astype(jnp.bfloat16)
        return gated_out.reshape(width_n, heads_here * head_size)

    gated_cols = lax.map(attend, jnp.arange(row_count, dtype=jnp.int32))
    returned = lax.all_to_all(
        gated_cols.reshape(row_count, -1), "dap", split_axis=1, concat_axis=0, tiled=True
    )
    returned = returned.reshape(width_n, row_count, heads_here * head_size)
    update = lax.psum_scatter(
        jnp.einsum("jic,cd->ijd", returned, w_out, preferred_element_type=jnp.float32),
        "heads",
        scatter_dimension=0,
        tiled=True,
    )
    return update.astype(jnp.bfloat16)


def fits(mesh, pair, w_bias):
    n, groups = mesh.shape["dap"], mesh.shape["heads"]
    rows, width, channels = pair.shape
    devices = n * groups
    heads = w_bias.shape[1] * groups
    return (
        groups == 2
        and channels == 128
        and width <= 128
        and width % devices == 0
        and width % 32 == 0
        and n % 8 == 0
        and rows % groups == 0
    )


def solution(mesh):
    n, groups = mesh.shape["dap"], mesh.shape["heads"]

    def run(pair, ln_gain, ln_shift, w_project, w_bias, w_out):
        if fits(mesh, pair, w_bias):
            return fused(n, groups, pair, ln_gain, ln_shift, w_project, w_bias, w_out)
        return local(pair, ln_gain, ln_shift, w_project, w_bias, w_out)

    in_specs = (
        P("dap", None, None),
        P(),
        P(),
        P(None, None, "heads"),
        P(None, "heads"),
        P("heads", None),
    )
    out_specs = P(("dap", "heads"), None, None)
    return jax.shard_map(run, mesh=mesh, in_specs=in_specs, out_specs=out_specs, check_vma=False)
```

```python
import functools
import math

import jax
import jax.numpy as jnp
from jax import lax
from jax.experimental import pallas as pl
from jax.experimental.pallas import tpu as pltpu
from jax.sharding import PartitionSpec as P

MESH = pl.DeviceIdType.MESH
F32 = jnp.float32
BF16 = jnp.bfloat16
NT = (((1,), (1,)), ((), ()))
VMEM_BYTES = 60 * 1024 * 1024


def up(size, unit):
    return -(-size // unit) * unit


def nt_dot(left, right):
    return lax.dot_general(left, right, NT, preferred_element_type=F32)


def kernel(
    dims,
    pair_hbm,
    gain_hbm,
    shift_hbm,
    bias_hbm,
    project_hbm,
    w_out_hbm,
    out_ref,
    pair_ref,
    gain_ref,
    shift_ref,
    bias_ref,
    normed,
    stage,
    x_send,
    x_recv,
    tokens,
    w_all,
    b_pad,
    b_recv,
    bias,
    gated,
    g_stage,
    g_send,
    g_recv,
    projected,
    load_sem,
    w_send_sem,
    w_recv_sem,
    x_send_sem,
    x_recv_sem,
    b_send_sem,
    b_recv_sem,
    g_send_sem,
    g_recv_sem,
):
    n, groups, rows, width, cols, heads, size = dims
    own_heads = heads // groups
    inner = own_heads * size
    devices = n * groups
    own_rows = rows // groups
    d = lax.axis_index("dap")
    g = lax.axis_index("heads")
    me = g * n + d
    quad = min(4, n)
    slabs = n // quad
    z, r = d // quad, lax.rem(d, quad)
    planes = [g, 1 - g]
    dap_at = [lax.rem(d + offset, n) for offset in range(n)]
    slab_at = [lax.rem(z + back, slabs) * quad for back in range(slabs)]
    near_at = [lax.rem(r + near, quad) for near in range(quad)]

    low_out = 4 * inner
    loads = [
        pltpu.make_async_copy(pair_hbm, pair_ref, load_sem.at[0]),
        pltpu.make_async_copy(gain_hbm, gain_ref, load_sem.at[4]),
        pltpu.make_async_copy(shift_hbm, shift_ref, load_sem.at[5]),
    ]
    w_loads = [
        pltpu.make_async_copy(bias_hbm, bias_ref, load_sem.at[1]),
        pltpu.make_async_copy(project_hbm, w_all.at[g, pl.ds(0, low_out)], load_sem.at[2]),
        pltpu.make_async_copy(w_out_hbm, w_all.at[g, pl.ds(low_out, inner)], load_sem.at[3]),
    ]
    for copy in loads + w_loads:
        copy.start()

    barrier = pltpu.get_barrier_semaphore()
    others = [(k % n, k // n) for k in range(1, devices)]
    for offset, plane in others:
        pl.semaphore_signal(
            barrier, inc=1, device_id=(dap_at[offset], planes[plane]), device_id_type=MESH
        )

    for copy in loads:
        copy.wait()
    gain = gain_ref[...]
    shift = shift_ref[...]
    for a in range(rows):
        values = pair_ref[a].astype(F32)
        average = jnp.mean(values, axis=-1, keepdims=True)
        centred = values - average
        variance = jnp.mean(centred * centred, axis=-1, keepdims=True)
        normed[a * width : (a + 1) * width, :] = (
            centred * lax.rsqrt(variance + 1e-05) * gain + shift
        )

    x_used = x_send.shape[1]
    x_rows = up(x_used, 8)
    for a in range(rows):
        for c in range(cols):
            start = pl.multiple_of(a * width + c * devices + g * n, 8)
            stage[pl.ds(a * cols + c, n, x_rows), :] = normed[pl.ds(start, n), :]
    x_send[...] = stage[...].reshape(n, x_rows, -1)[:, :x_used].astype(BF16)

    w_loads[0].wait()
    b_pad[0:own_heads, :] = bias_ref[...]
    w_bias = b_pad[...]
    for a in range(rows):
        part = nt_dot(w_bias, normed[a * width : (a + 1) * width, :].astype(BF16))
        for h in range(own_heads):
            row = h * rows + a
            b_recv[d, g, row : row + 1, 0:width] = part[h : h + 1]
    for copy in w_loads[1:]:
        copy.wait()

    pl.semaphore_wait(barrier, devices - 1)

    def send(src, dst, send_sem, recv_sem, other, plane=g):
        copy = pltpu.make_async_remote_copy(
            src_ref=src,
            dst_ref=dst,
            send_sem=send_sem,
            recv_sem=recv_sem,
            device_id=(other, plane),
            device_id_type=MESH,
        )
        copy.start()
        return copy

    def drain(ref, sem):
        pltpu.make_async_copy(ref, ref, sem).wait()

    b_used = own_heads * rows
    own_bias = b_recv.at[d, g, pl.ds(0, b_used)]
    first = [(back, plane) for plane in range(groups) for back in range(slabs)][1:]
    across = {}
    for back, plane in first:
        k = back * groups + plane
        across[back, plane] = send(
            own_bias, own_bias, b_send_sem.at[0], b_recv_sem.at[k], slab_at[back] + r, planes[plane]
        )

    far = [near + back * quad for back in range(1, slabs) for near in range(quad)]
    for offset in far + list(range(1, quad)):
        other = slab_at[offset // quad] + near_at[offset % quad]
        send(x_send.at[other], x_recv.at[d], x_send_sem, x_recv_sem, other)
    own_w = w_all.at[g]
    w_copy = send(own_w, own_w, w_send_sem, w_recv_sem, d, planes[1])
    x_recv[d] = x_send[d]

    for back in range(slabs):
        for plane in range(groups):
            if back or plane:
                across[back, plane].wait_recv()
        block = slab_at[(slabs - back) % slabs] + r
        both = b_recv.at[block, :, pl.ds(0, b_used)]
        for near in range(1, quad):
            send(both, both, b_send_sem.at[1], b_recv_sem.at[0], slab_at[0] + near_at[near])

    drain(x_recv.at[pl.ds(0, n - 1)], x_recv_sem)
    for k in range(n):
        stage[k * x_rows : k * x_rows + x_used, :] = x_recv[k].astype(F32)
    for a in range(rows):
        for c in range(cols):
            tokens[pl.ds(c * width + a, n, rows), :] = stage[pl.ds(a * cols + c, n, x_rows), :]
    entries = tokens[...].astype(BF16)

    w_copy.wait_recv()

    def weight(t):
        low = t * inner
        return jnp.concatenate([w_all[k, low : low + inner, :] for k in range(groups)], axis=0)

    queries = nt_dot(entries, weight(0)).astype(BF16)
    keys = nt_dot(entries, weight(1)).astype(BF16)
    w_value, w_gate = weight(2), weight(3)
    lane = lax.broadcasted_iota(jnp.int32, (width, heads * size), 1) // size
    scores, values, gating = [], [], []
    for c in range(cols):
        part = slice(c * width, (c + 1) * width)
        key = keys[part]
        stacked = jnp.concatenate(
            [jnp.where(lane == h, key, jnp.zeros_like(key)) for h in range(heads)], axis=0
        )
        scores.append(nt_dot(stacked, queries[part]))
        values.append(nt_dot(w_value, entries[part]).astype(BF16))
        gating.append(jax.nn.sigmoid(nt_dot(w_gate, entries[part])).astype(BF16).astype(F32))

    passed = slabs * (quad - 1)
    drain(b_recv.at[pl.ds(0, passed), :, pl.ds(0, b_used)], b_recv_sem.at[0])
    b_rows = b_recv.shape[2]
    gathered = b_recv.reshape(n * groups * b_rows, 128)
    for h in range(heads):
        for a in range(rows):
            first_row = h // own_heads * b_rows + h % own_heads * rows + a
            bias[pl.ds(h * width + a, n, rows), :] = gathered[
                pl.ds(first_row, n, groups * b_rows), :
            ]

    scale = 1.0 / math.sqrt(size)
    for c in range(cols):
        parts = []
        for h in range(heads):
            part = slice(h * width, (h + 1) * width)
            score = scores[c][part] * scale + bias[part, 0:width]
            exponent = jnp.exp(score - jnp.max(score, axis=0, keepdims=True))
            total = jnp.sum(exponent, axis=0, keepdims=True)
            head = slice(h * size, (h + 1) * size)
            attended = jnp.dot(values[c][head], exponent.astype(BF16), preferred_element_type=F32)
            parts.append(attended / total * gating[c][head])
        gated[c * width : (c + 1) * width, :] = jnp.concatenate(parts, axis=0).T

    g_used = g_send.shape[1]
    g_rows = up(g_used, 8)
    for i in range(own_rows):
        for c in range(cols):
            g_stage[pl.ds(i * cols + c, devices, g_rows), :] = gated[
                pl.ds(c * width + i, devices, own_rows), :
            ]
    g_send[...] = g_stage[...].reshape(devices, g_rows, -1)[:, :g_used].astype(BF16)

    for offset, plane in sorted(others, key=lambda o: -min(o[0], n - o[0])):
        other_d, other_g = dap_at[offset], planes[plane]
        send(
            g_send.at[other_d * groups + other_g],
            g_recv.at[me],
            g_send_sem,
            g_recv_sem,
            other_d,
            other_g,
        )
    g_recv[me] = g_send[d * groups + g]
    drain(b_recv.at[pl.ds(0, len(first)), 0, pl.ds(0, b_used)], b_send_sem.at[0])
    drain(b_recv.at[pl.ds(0, passed), :, pl.ds(0, b_used)], b_send_sem.at[1])
    drain(x_send.at[pl.ds(0, n - 1)], x_send_sem)
    w_copy.wait_send()
    drain(g_send.at[pl.ds(0, devices - 1)], g_send_sem)
    w_out = jnp.concatenate([w_all[k, low_out : low_out + inner, :] for k in range(groups)], axis=0)
    drain(g_recv.at[pl.ds(0, devices - 1)], g_recv_sem)
    for k in range(devices):
        g_stage[k * g_rows : k * g_rows + g_used, :] = g_recv[k].astype(F32)
    projected[...] = jnp.dot(g_stage[...].astype(BF16), w_out, preferred_element_type=F32)
    for i in range(own_rows):
        for c in range(cols):
            out_ref[i, c * devices : (c + 1) * devices, :] = projected[
                pl.ds(i * cols + c, devices, g_rows), :
            ].astype(BF16)


def fused(n, groups, pair, ln_gain, ln_shift, w_project, w_bias, w_out):
    rows, width, channels = pair.shape
    own_heads = w_bias.shape[1]
    heads = own_heads * groups
    size = w_project.shape[2] // own_heads
    devices = n * groups
    cols = width // devices
    own_rows = rows // groups
    inner = own_heads * size
    w_rows = 5 * inner
    b_rows = up(own_heads * rows, 8)
    x_used = up(rows * cols, 2)
    x_rows = up(x_used, 8)
    g_used = up(own_rows * cols, 2)
    g_rows = up(g_used, 8)
    dims = (n, groups, rows, width, cols, heads, size)
    vmem = pl.BlockSpec(memory_space=pltpu.VMEM)
    hbm = pl.BlockSpec(memory_space=pl.ANY)
    sems = pltpu.SemaphoreType.DMA
    return pl.pallas_call(
        functools.partial(kernel, dims),
        out_shape=pltpu.VMEM((own_rows, width, channels), BF16),
        in_specs=[hbm] * 6,
        out_specs=vmem,
        scratch_shapes=[
            pltpu.VMEM((rows, width, channels), BF16),
            pltpu.VMEM((1, channels), F32),
            pltpu.VMEM((1, channels), F32),
            pltpu.VMEM((own_heads, channels), BF16),
            pltpu.VMEM((rows * width, channels), F32),
            pltpu.VMEM((n * x_rows, channels), F32),
            pltpu.VMEM((n, x_used, channels), BF16),
            pltpu.VMEM((n, x_used, channels), BF16),
            pltpu.VMEM((cols * width, channels), F32),
            pltpu.VMEM((groups, w_rows, channels), BF16),
            pltpu.VMEM((16, channels), BF16),
            pltpu.VMEM((n, groups, b_rows, 128), F32),
            pltpu.VMEM((heads * width, 128), F32),
            pltpu.VMEM((cols * width, heads * size), F32),
            pltpu.VMEM((devices * g_rows, heads * size), F32),
            pltpu.VMEM((devices, g_used, heads * size), BF16),
            pltpu.VMEM((devices, g_used, heads * size), BF16),
            pltpu.VMEM((devices * g_rows, channels), F32),
            sems((6,)),
            sems(()),
            sems(()),
            sems(()),
            sems(()),
            sems((2,)),
            sems((n // min(4, n) * groups,)),
            sems(()),
            sems(()),
        ],
        compiler_params=pltpu.CompilerParams(
            collective_id=0, has_side_effects=True, vmem_limit_bytes=VMEM_BYTES
        ),
    )(
        pair,
        ln_gain.reshape(1, -1),
        ln_shift.reshape(1, -1),
        w_bias.T,
        jnp.transpose(w_project, (1, 2, 0)).reshape(-1, channels),
        w_out,
    )


def normalize(pair, ln_gain, ln_shift):
    values_f = pair.astype(jnp.float32)
    average = jnp.mean(values_f, axis=-1, keepdims=True)
    centred = values_f - average
    variance = jnp.mean(centred * centred, axis=-1, keepdims=True)
    return (centred * lax.rsqrt(variance + 1e-05) * ln_gain + ln_shift).astype(jnp.bfloat16)


def project_entries(normed, flat_w):
    projected = jnp.dot(normed, flat_w, preferred_element_type=jnp.float32)
    head_width = flat_w.shape[1] // 4
    head_part = projected[..., : 3 * head_width].astype(jnp.bfloat16)
    gating = jax.nn.sigmoid(projected[..., 3 * head_width :]).astype(jnp.bfloat16)
    return jnp.concatenate([head_part, gating], axis=-1)


def local(pair, ln_gain, ln_shift, w_project, w_bias, w_out):
    row_count, width_n, channels = pair.shape
    heads_here = w_bias.shape[1]
    head_size = w_project.shape[2] // heads_here
    flat_w = w_project.reshape(channels, -1)
    normed_rows = normalize(pair, ln_gain, ln_shift)
    bias_rows = jnp.einsum("abc,ch->hab", normed_rows, w_bias, preferred_element_type=jnp.float32)
    bias_all = lax.all_gather(bias_rows, "dap", axis=1, tiled=True)
    bias_key_last = jnp.swapaxes(bias_all, 1, 2)
    dap_count = lax.axis_size("dap")
    blocks = pair.reshape(row_count, dap_count, width_n // dap_count, channels)
    packed = project_entries(
        normalize(
            lax.all_to_all(blocks, "dap", split_axis=1, concat_axis=0, tiled=True),
            ln_gain,
            ln_shift,
        ),
        flat_w,
    )
    packed = packed.reshape(width_n, row_count, -1)

    def attend(index):
        column_data = lax.dynamic_index_in_dim(packed, index, 1, keepdims=False)
        pieces = column_data.reshape(width_n, 4, heads_here, head_size)
        scores = jnp.einsum(
            "ihc,khc->hik", pieces[:, 0], pieces[:, 1], preferred_element_type=jnp.float32
        )
        scores = scores * (1.0 / math.sqrt(head_size)) + bias_key_last
        highest = jnp.max(scores, axis=-1, keepdims=True)
        exponent = jnp.exp(scores - highest)
        totals = jnp.sum(exponent, axis=-1)
        weights = exponent.astype(jnp.bfloat16)
        attended = jnp.einsum(
            "hik,khc->ihc", weights, pieces[:, 2], preferred_element_type=jnp.float32
        )
        attended = attended / jnp.swapaxes(totals, 0, 1)[..., None]
        gated_out = (attended * pieces[:, 3].astype(jnp.float32)).astype(jnp.bfloat16)
        return gated_out.reshape(width_n, heads_here * head_size)

    gated_cols = lax.map(attend, jnp.arange(row_count, dtype=jnp.int32))
    returned = lax.all_to_all(
        gated_cols.reshape(row_count, -1), "dap", split_axis=1, concat_axis=0, tiled=True
    )
    returned = returned.reshape(width_n, row_count, heads_here * head_size)
    update = lax.psum_scatter(
        jnp.einsum("jic,cd->ijd", returned, w_out, preferred_element_type=jnp.float32),
        "heads",
        scatter_dimension=0,
        tiled=True,
    )
    return update.astype(jnp.bfloat16)


def fits(mesh, pair, w_bias):
    n, groups = mesh.shape["dap"], mesh.shape["heads"]
    rows, width, channels = pair.shape
    devices = n * groups
    heads = w_bias.shape[1] * groups
    return (
        groups == 2
        and channels == 128
        and width <= 128
        and width % devices == 0
        and width % 32 == 0
        and n % 8 == 0
        and rows % groups == 0
    )


def solution(mesh):
    n, groups = mesh.shape["dap"], mesh.shape["heads"]

    def run(pair, ln_gain, ln_shift, w_project, w_bias, w_out):
        if fits(mesh, pair, w_bias):
            return fused(n, groups, pair, ln_gain, ln_shift, w_project, w_bias, w_out)
        return local(pair, ln_gain, ln_shift, w_project, w_bias, w_out)

    in_specs = (
        P("dap", None, None),
        P(),
        P(),
        P(None, None, "heads"),
        P(None, "heads"),
        P("heads", None),
    )
    out_specs = P(("dap", "heads"), None, None)
    return jax.shard_map(run, mesh=mesh, in_specs=in_specs, out_specs=out_specs, check_vma=False)
```

```python
import functools
import math

import jax
import jax.numpy as jnp
from jax import lax
from jax.experimental import pallas as pl
from jax.experimental.pallas import tpu as pltpu
from jax.sharding import PartitionSpec as P

MESH = pl.DeviceIdType.MESH
F32 = jnp.float32
BF16 = jnp.bfloat16
NT = (((1,), (1,)), ((), ()))
VMEM_BYTES = 60 * 1024 * 1024


def up(size, unit):
    return -(-size // unit) * unit


def nt_dot(left, right):
    return lax.dot_general(left, right, NT, preferred_element_type=F32)


def kernel(
    dims,
    pair_hbm,
    gain_hbm,
    shift_hbm,
    bias_hbm,
    project_hbm,
    w_out_hbm,
    out_ref,
    pair_ref,
    gain_ref,
    shift_ref,
    bias_ref,
    normed,
    stage,
    x_send,
    x_recv,
    tokens,
    w_all,
    b_pad,
    b_recv,
    bias,
    gated,
    g_stage,
    g_send,
    g_recv,
    projected,
    load_sem,
    w_send_sem,
    w_recv_sem,
    x_send_sem,
    x_recv_sem,
    b_send_sem,
    b_recv_sem,
    g_send_sem,
    g_recv_sem,
):
    n, groups, rows, width, cols, heads, size = dims
    own_heads = heads // groups
    inner = own_heads * size
    devices = n * groups
    own_rows = rows // groups
    d = lax.axis_index("dap")
    g = lax.axis_index("heads")
    me = g * n + d
    quad = min(4, n)
    slabs = n // quad
    z, r = d // quad, lax.rem(d, quad)
    planes = [g, 1 - g]
    dap_at = [lax.rem(d + offset, n) for offset in range(n)]
    slab_at = [lax.rem(z + back, slabs) * quad for back in range(slabs)]
    near_at = [lax.rem(r + near, quad) for near in range(quad)]

    low_out = 4 * inner
    loads = [
        pltpu.make_async_copy(pair_hbm, pair_ref, load_sem.at[0]),
        pltpu.make_async_copy(gain_hbm, gain_ref, load_sem.at[4]),
        pltpu.make_async_copy(shift_hbm, shift_ref, load_sem.at[5]),
    ]
    w_loads = [
        pltpu.make_async_copy(bias_hbm, bias_ref, load_sem.at[1]),
        pltpu.make_async_copy(project_hbm, w_all.at[g, pl.ds(0, low_out)], load_sem.at[2]),
        pltpu.make_async_copy(w_out_hbm, w_all.at[g, pl.ds(low_out, inner)], load_sem.at[3]),
    ]
    for copy in loads + w_loads:
        copy.start()

    barrier = pltpu.get_barrier_semaphore()
    others = [(k % n, k // n) for k in range(1, devices)]
    for offset, plane in others:
        pl.semaphore_signal(
            barrier, inc=1, device_id=(dap_at[offset], planes[plane]), device_id_type=MESH
        )

    for copy in loads:
        copy.wait()
    gain = gain_ref[...]
    shift = shift_ref[...]
    for a in range(rows):
        values = pair_ref[a].astype(F32)
        average = jnp.mean(values, axis=-1, keepdims=True)
        centred = values - average
        variance = jnp.mean(centred * centred, axis=-1, keepdims=True)
        normed[a * width : (a + 1) * width, :] = (
            centred * lax.rsqrt(variance + 1e-05) * gain + shift
        )

    x_rows = x_send.shape[1]
    for a in range(rows):
        for c in range(cols):
            start = pl.multiple_of(a * width + c * devices + g * n, 8)
            stage[pl.ds(a * cols + c, n, x_rows), :] = normed[pl.ds(start, n), :]
    x_send[...] = stage[...].reshape(n, x_rows, -1).astype(BF16)

    w_loads[0].wait()
    b_pad[0:own_heads, :] = bias_ref[...]
    w_bias = b_pad[...]
    for a in range(rows):
        part = nt_dot(w_bias, normed[a * width : (a + 1) * width, :].astype(BF16))
        for h in range(own_heads):
            row = h * rows + a
            b_recv[d, g, row : row + 1, 0:width] = part[h : h + 1]
    for copy in w_loads[1:]:
        copy.wait()

    pl.semaphore_wait(barrier, devices - 1)

    def send(src, dst, send_sem, recv_sem, other, plane=g):
        copy = pltpu.make_async_remote_copy(
            src_ref=src,
            dst_ref=dst,
            send_sem=send_sem,
            recv_sem=recv_sem,
            device_id=(other, plane),
            device_id_type=MESH,
        )
        copy.start()
        return copy

    def drain(ref, sem):
        pltpu.make_async_copy(ref, ref, sem).wait()

    own_bias = b_recv.at[d, g]
    first = [(back, plane) for plane in range(groups) for back in range(slabs)][1:]
    across = {}
    for back, plane in first:
        k = back * groups + plane
        across[back, plane] = send(
            own_bias, own_bias, b_send_sem.at[0], b_recv_sem.at[k], slab_at[back] + r, planes[plane]
        )

    far = [near + back * quad for back in range(1, slabs) for near in range(quad)]
    for offset in far + list(range(1, quad)):
        other = slab_at[offset // quad] + near_at[offset % quad]
        send(x_send.at[other], x_recv.at[d], x_send_sem, x_recv_sem, other)
    own_w = w_all.at[g]
    w_copy = send(own_w, own_w, w_send_sem, w_recv_sem, d, planes[1])
    x_recv[d] = x_send[d]

    for back in range(slabs):
        for plane in range(groups):
            if back or plane:
                across[back, plane].wait_recv()
        block = slab_at[(slabs - back) % slabs] + r
        both = b_recv.at[block]
        for near in range(1, quad):
            send(both, both, b_send_sem.at[1], b_recv_sem.at[0], slab_at[0] + near_at[near])

    drain(x_recv.at[pl.ds(0, n - 1)], x_recv_sem)
    stage[...] = x_recv[...].reshape(n * x_rows, -1).astype(F32)
    for a in range(rows):
        for c in range(cols):
            tokens[pl.ds(c * width + a, n, rows), :] = stage[pl.ds(a * cols + c, n, x_rows), :]
    entries = tokens[...].astype(BF16)

    w_copy.wait_recv()

    def weight(t):
        low = t * inner
        return jnp.concatenate([w_all[k, low : low + inner, :] for k in range(groups)], axis=0)

    queries = nt_dot(entries, weight(0)).astype(BF16)
    keys = nt_dot(entries, weight(1)).astype(BF16)
    w_value, w_gate = weight(2), weight(3)
    lane = lax.broadcasted_iota(jnp.int32, (width, heads * size), 1) // size
    scores, values, gating = [], [], []
    for c in range(cols):
        part = slice(c * width, (c + 1) * width)
        key = keys[part]
        stacked = jnp.concatenate(
            [jnp.where(lane == h, key, jnp.zeros_like(key)) for h in range(heads)], axis=0
        )
        scores.append(nt_dot(stacked, queries[part]))
        values.append(nt_dot(w_value, entries[part]).astype(BF16))
        gating.append(jax.nn.sigmoid(nt_dot(w_gate, entries[part])).astype(BF16).astype(F32))

    passed = slabs * (quad - 1)
    drain(b_recv.at[pl.ds(0, passed)], b_recv_sem.at[0])
    b_rows = b_recv.shape[2]
    gathered = b_recv.reshape(n * groups * b_rows, 128)
    for h in range(heads):
        for a in range(rows):
            first_row = h // own_heads * b_rows + h % own_heads * rows + a
            bias[pl.ds(h * width + a, n, rows), :] = gathered[
                pl.ds(first_row, n, groups * b_rows), :
            ]

    scale = 1.0 / math.sqrt(size)
    for c in range(cols):
        parts = []
        for h in range(heads):
            part = slice(h * width, (h + 1) * width)
            score = scores[c][part] * scale + bias[part, 0:width]
            exponent = jnp.exp(score - jnp.max(score, axis=0, keepdims=True))
            total = jnp.sum(exponent, axis=0, keepdims=True)
            head = slice(h * size, (h + 1) * size)
            attended = jnp.dot(values[c][head], exponent.astype(BF16), preferred_element_type=F32)
            parts.append(attended / total * gating[c][head])
        gated[c * width : (c + 1) * width, :] = jnp.concatenate(parts, axis=0).T

    g_rows = g_send.shape[1]
    for i in range(own_rows):
        for c in range(cols):
            g_stage[pl.ds(i * cols + c, devices, g_rows), :] = gated[
                pl.ds(c * width + i, devices, own_rows), :
            ]
    g_send[...] = g_stage[...].reshape(devices, g_rows, -1).astype(BF16)

    for offset, plane in sorted(others, key=lambda o: -min(o[0], n - o[0])):
        other_d, other_g = dap_at[offset], planes[plane]
        send(
            g_send.at[other_d * groups + other_g],
            g_recv.at[me],
            g_send_sem,
            g_recv_sem,
            other_d,
            other_g,
        )
    g_recv[me] = g_send[d * groups + g]
    drain(b_recv.at[pl.ds(0, len(first)), 0], b_send_sem.at[0])
    drain(b_recv.at[pl.ds(0, passed)], b_send_sem.at[1])
    drain(x_send.at[pl.ds(0, n - 1)], x_send_sem)
    w_copy.wait_send()
    drain(g_send.at[pl.ds(0, devices - 1)], g_send_sem)
    w_out = jnp.concatenate([w_all[k, low_out : low_out + inner, :] for k in range(groups)], axis=0)
    drain(g_recv.at[pl.ds(0, devices - 1)], g_recv_sem)
    projected[...] = jnp.dot(
        g_recv[...].reshape(devices * g_rows, -1), w_out, preferred_element_type=F32
    )
    for i in range(own_rows):
        for c in range(cols):
            out_ref[i, c * devices : (c + 1) * devices, :] = projected[
                pl.ds(i * cols + c, devices, g_rows), :
            ].astype(BF16)


def fused(n, groups, pair, ln_gain, ln_shift, w_project, w_bias, w_out):
    rows, width, channels = pair.shape
    own_heads = w_bias.shape[1]
    heads = own_heads * groups
    size = w_project.shape[2] // own_heads
    devices = n * groups
    cols = width // devices
    own_rows = rows // groups
    inner = own_heads * size
    w_rows = 5 * inner
    b_rows = up(own_heads * rows, 8)
    x_rows = up(rows * cols, 16)
    g_rows = up(own_rows * cols, 16)
    dims = (n, groups, rows, width, cols, heads, size)
    vmem = pl.BlockSpec(memory_space=pltpu.VMEM)
    hbm = pl.BlockSpec(memory_space=pl.ANY)
    sems = pltpu.SemaphoreType.DMA
    return pl.pallas_call(
        functools.partial(kernel, dims),
        out_shape=pltpu.VMEM((own_rows, width, channels), BF16),
        in_specs=[hbm] * 6,
        out_specs=vmem,
        scratch_shapes=[
            pltpu.VMEM((rows, width, channels), BF16),
            pltpu.VMEM((1, channels), F32),
            pltpu.VMEM((1, channels), F32),
            pltpu.VMEM((own_heads, channels), BF16),
            pltpu.VMEM((rows * width, channels), F32),
            pltpu.VMEM((n * x_rows, channels), F32),
            pltpu.VMEM((n, x_rows, channels), BF16),
            pltpu.VMEM((n, x_rows, channels), BF16),
            pltpu.VMEM((cols * width, channels), F32),
            pltpu.VMEM((groups, w_rows, channels), BF16),
            pltpu.VMEM((16, channels), BF16),
            pltpu.VMEM((n, groups, b_rows, 128), F32),
            pltpu.VMEM((heads * width, 128), F32),
            pltpu.VMEM((cols * width, heads * size), F32),
            pltpu.VMEM((devices * g_rows, heads * size), F32),
            pltpu.VMEM((devices, g_rows, heads * size), BF16),
            pltpu.VMEM((devices, g_rows, heads * size), BF16),
            pltpu.VMEM((devices * g_rows, channels), F32),
            sems((6,)),
            sems(()),
            sems(()),
            sems(()),
            sems(()),
            sems((2,)),
            sems((n // min(4, n) * groups,)),
            sems(()),
            sems(()),
        ],
        compiler_params=pltpu.CompilerParams(
            collective_id=0, has_side_effects=True, vmem_limit_bytes=VMEM_BYTES
        ),
    )(
        pair,
        ln_gain.reshape(1, -1),
        ln_shift.reshape(1, -1),
        w_bias.T,
        jnp.transpose(w_project, (1, 2, 0)).reshape(-1, channels),
        w_out,
    )


def normalize(pair, ln_gain, ln_shift):
    values_f = pair.astype(jnp.float32)
    average = jnp.mean(values_f, axis=-1, keepdims=True)
    centred = values_f - average
    variance = jnp.mean(centred * centred, axis=-1, keepdims=True)
    return (centred * lax.rsqrt(variance + 1e-05) * ln_gain + ln_shift).astype(jnp.bfloat16)


def project_entries(normed, flat_w):
    projected = jnp.dot(normed, flat_w, preferred_element_type=jnp.float32)
    head_width = flat_w.shape[1] // 4
    head_part = projected[..., : 3 * head_width].astype(jnp.bfloat16)
    gating = jax.nn.sigmoid(projected[..., 3 * head_width :]).astype(jnp.bfloat16)
    return jnp.concatenate([head_part, gating], axis=-1)


def local(pair, ln_gain, ln_shift, w_project, w_bias, w_out):
    row_count, width_n, channels = pair.shape
    heads_here = w_bias.shape[1]
    head_size = w_project.shape[2] // heads_here
    flat_w = w_project.reshape(channels, -1)
    normed_rows = normalize(pair, ln_gain, ln_shift)
    bias_rows = jnp.einsum("abc,ch->hab", normed_rows, w_bias, preferred_element_type=jnp.float32)
    bias_all = lax.all_gather(bias_rows, "dap", axis=1, tiled=True)
    bias_key_last = jnp.swapaxes(bias_all, 1, 2)
    dap_count = lax.axis_size("dap")
    blocks = pair.reshape(row_count, dap_count, width_n // dap_count, channels)
    packed = project_entries(
        normalize(
            lax.all_to_all(blocks, "dap", split_axis=1, concat_axis=0, tiled=True),
            ln_gain,
            ln_shift,
        ),
        flat_w,
    )
    packed = packed.reshape(width_n, row_count, -1)

    def attend(index):
        column_data = lax.dynamic_index_in_dim(packed, index, 1, keepdims=False)
        pieces = column_data.reshape(width_n, 4, heads_here, head_size)
        scores = jnp.einsum(
            "ihc,khc->hik", pieces[:, 0], pieces[:, 1], preferred_element_type=jnp.float32
        )
        scores = scores * (1.0 / math.sqrt(head_size)) + bias_key_last
        highest = jnp.max(scores, axis=-1, keepdims=True)
        exponent = jnp.exp(scores - highest)
        totals = jnp.sum(exponent, axis=-1)
        weights = exponent.astype(jnp.bfloat16)
        attended = jnp.einsum(
            "hik,khc->ihc", weights, pieces[:, 2], preferred_element_type=jnp.float32
        )
        attended = attended / jnp.swapaxes(totals, 0, 1)[..., None]
        gated_out = (attended * pieces[:, 3].astype(jnp.float32)).astype(jnp.bfloat16)
        return gated_out.reshape(width_n, heads_here * head_size)

    gated_cols = lax.map(attend, jnp.arange(row_count, dtype=jnp.int32))
    returned = lax.all_to_all(
        gated_cols.reshape(row_count, -1), "dap", split_axis=1, concat_axis=0, tiled=True
    )
    returned = returned.reshape(width_n, row_count, heads_here * head_size)
    update = lax.psum_scatter(
        jnp.einsum("jic,cd->ijd", returned, w_out, preferred_element_type=jnp.float32),
        "heads",
        scatter_dimension=0,
        tiled=True,
    )
    return update.astype(jnp.bfloat16)


def fits(mesh, pair, w_bias):
    n, groups = mesh.shape["dap"], mesh.shape["heads"]
    rows, width, channels = pair.shape
    devices = n * groups
    heads = w_bias.shape[1] * groups
    return (
        groups == 2
        and channels == 128
        and width <= 128
        and width % devices == 0
        and width % 32 == 0
        and n % 8 == 0
        and rows % groups == 0
    )


def solution(mesh):
    n, groups = mesh.shape["dap"], mesh.shape["heads"]

    def run(pair, ln_gain, ln_shift, w_project, w_bias, w_out):
        if fits(mesh, pair, w_bias):
            return fused(n, groups, pair, ln_gain, ln_shift, w_project, w_bias, w_out)
        return local(pair, ln_gain, ln_shift, w_project, w_bias, w_out)

    in_specs = (
        P("dap", None, None),
        P(),
        P(),
        P(None, None, "heads"),
        P(None, "heads"),
        P("heads", None),
    )
    out_specs = P(("dap", "heads"), None, None)
    return jax.shard_map(run, mesh=mesh, in_specs=in_specs, out_specs=out_specs, check_vma=False)
```

```python
import functools
import math

import jax
import jax.numpy as jnp
from jax import lax
from jax.experimental import pallas as pl
from jax.experimental.pallas import tpu as pltpu
from jax.sharding import PartitionSpec as P

MESH = pl.DeviceIdType.MESH
F32 = jnp.float32
BF16 = jnp.bfloat16
NT = (((1,), (1,)), ((), ()))
VMEM_BYTES = 60 * 1024 * 1024


def up(size, unit):
    return -(-size // unit) * unit


def nt_dot(left, right):
    return lax.dot_general(left, right, NT, preferred_element_type=F32)


def kernel(
    dims,
    pair_hbm,
    gain_hbm,
    shift_hbm,
    bias_hbm,
    project_hbm,
    w_out_hbm,
    out_ref,
    pair_ref,
    gain_ref,
    shift_ref,
    bias_ref,
    normed,
    stage,
    x_send,
    x_recv,
    tokens,
    w_all,
    b_pad,
    b_recv,
    bias,
    gated,
    g_stage,
    g_send,
    g_recv,
    projected,
    load_sem,
    w_send_sem,
    w_recv_sem,
    x_send_sem,
    x_recv_sem,
    b_send_sem,
    b_recv_sem,
    g_send_sem,
    g_recv_sem,
):
    n, groups, rows, width, cols, heads, size = dims
    own_heads = heads // groups
    inner = own_heads * size
    devices = n * groups
    own_rows = rows // groups
    d = lax.axis_index("dap")
    g = lax.axis_index("heads")
    me = g * n + d
    quad = min(4, n)
    slabs = n // quad
    z, r = d // quad, lax.rem(d, quad)
    planes = [g, 1 - g]
    dap_at = [lax.rem(d + offset, n) for offset in range(n)]
    slab_at = [lax.rem(z + back, slabs) * quad for back in range(slabs)]
    near_at = [lax.rem(r + near, quad) for near in range(quad)]

    low_out = 4 * inner
    loads = [
        pltpu.make_async_copy(pair_hbm, pair_ref, load_sem.at[0]),
        pltpu.make_async_copy(gain_hbm, gain_ref, load_sem.at[4]),
        pltpu.make_async_copy(shift_hbm, shift_ref, load_sem.at[5]),
    ]
    w_loads = [
        pltpu.make_async_copy(bias_hbm, bias_ref, load_sem.at[1]),
        pltpu.make_async_copy(project_hbm, w_all.at[g, pl.ds(0, low_out)], load_sem.at[2]),
        pltpu.make_async_copy(w_out_hbm, w_all.at[g, pl.ds(low_out, inner)], load_sem.at[3]),
    ]
    for copy in loads + w_loads:
        copy.start()

    barrier = pltpu.get_barrier_semaphore()
    others = [(k % n, k // n) for k in range(1, devices)]
    for offset, plane in others:
        pl.semaphore_signal(
            barrier, inc=1, device_id=(dap_at[offset], planes[plane]), device_id_type=MESH
        )

    for copy in loads:
        copy.wait()
    gain = gain_ref[...]
    shift = shift_ref[...]
    for a in range(rows):
        values = pair_ref[a].astype(F32)
        average = jnp.mean(values, axis=-1, keepdims=True)
        centred = values - average
        variance = jnp.mean(centred * centred, axis=-1, keepdims=True)
        normed[a * 128 : a * 128 + width, :] = (
            centred * lax.rsqrt(variance + 1e-05) * gain + shift
        )

    x_rows = x_send.shape[1]
    for a in range(rows):
        for c in range(cols):
            start = pl.multiple_of(a * 128 + c * devices + g * n, 8)
            stage[pl.ds(a * cols + c, n, x_rows), :] = normed[pl.ds(start, n), :]
    x_send[...] = stage[...].reshape(n, x_rows, -1).astype(BF16)

    w_loads[0].wait()
    b_pad[0:own_heads, :] = bias_ref[...]
    w_bias = b_pad[...]
    part = nt_dot(w_bias, normed[...].astype(BF16))
    for a in range(rows):
        for h in range(own_heads):
            row = h * rows + a
            b_recv[d, g, row : row + 1, :] = part[h : h + 1, a * 128 : (a + 1) * 128]
    for c in range(cols):
        tokens[c * 128 + width : (c + 1) * 128, :] = jnp.zeros((128 - width, 128), F32)
    for copy in w_loads[1:]:
        copy.wait()

    pl.semaphore_wait(barrier, devices - 1)

    def send(src, dst, send_sem, recv_sem, other, plane=g):
        copy = pltpu.make_async_remote_copy(
            src_ref=src,
            dst_ref=dst,
            send_sem=send_sem,
            recv_sem=recv_sem,
            device_id=(other, plane),
            device_id_type=MESH,
        )
        copy.start()
        return copy

    def drain(ref, sem):
        pltpu.make_async_copy(ref, ref, sem).wait()

    b_used = own_heads * rows
    own_bias = b_recv.at[d, g, pl.ds(0, b_used)]
    first = [(back, plane) for plane in range(groups) for back in range(slabs)][1:]
    across = {}
    for back, plane in first:
        k = back * groups + plane
        across[back, plane] = send(
            own_bias, own_bias, b_send_sem.at[0], b_recv_sem.at[k], slab_at[back] + r, planes[plane]
        )

    far = [near + back * quad for back in range(1, slabs) for near in range(quad)]
    for offset in far + list(range(1, quad)):
        other = slab_at[offset // quad] + near_at[offset % quad]
        send(x_send.at[other], x_recv.at[d], x_send_sem, x_recv_sem, other)
    own_w = w_all.at[g]
    w_copy = send(own_w, own_w, w_send_sem, w_recv_sem, d, planes[1])
    x_recv[d] = x_send[d]

    for back in range(slabs):
        for plane in range(groups):
            if back or plane:
                across[back, plane].wait_recv()
        block = slab_at[(slabs - back) % slabs] + r
        both = b_recv.at[block, :, pl.ds(0, b_used)]
        for near in range(1, quad):
            send(both, both, b_send_sem.at[1], b_recv_sem.at[0], slab_at[0] + near_at[near])

    drain(x_recv.at[pl.ds(0, n - 1)], x_recv_sem)
    stage[...] = x_recv[...].reshape(n * x_rows, -1).astype(F32)
    for a in range(rows):
        for c in range(cols):
            tokens[pl.ds(c * 128 + a, n, rows), :] = stage[pl.ds(a * cols + c, n, x_rows), :]
    entries = tokens[...].astype(BF16)

    w_copy.wait_recv()

    def weight(t):
        low = t * inner
        return jnp.concatenate([w_all[k, low : low + inner, :] for k in range(groups)], axis=0)

    keys = nt_dot(entries, weight(1)).astype(BF16)
    channels = heads * size
    w_rest = jnp.concatenate([weight(0), weight(2), weight(3)], axis=0)
    rest = nt_dot(w_rest, entries)
    queries = rest[:channels].astype(BF16)
    all_values = rest[channels : 2 * channels].astype(BF16)
    gating = jax.nn.sigmoid(rest[2 * channels :]).astype(BF16).astype(F32)
    lane = lax.broadcasted_iota(jnp.int32, (width, channels), 1) // size
    row = lax.broadcasted_iota(jnp.int32, (channels, 128), 0) // size
    scores, values = [], []
    for c in range(cols):
        key = keys[c * 128 : c * 128 + width]
        stacked = jnp.concatenate(
            [jnp.where(lane == h, key, jnp.zeros_like(key)) for h in range(heads)], axis=0
        )
        part = slice(c * 128, (c + 1) * 128)
        scores.append(jnp.dot(stacked, queries[:, part], preferred_element_type=F32))
        value = all_values[:, part]
        values.append(
            jnp.concatenate(
                [jnp.where(row == h, value, jnp.zeros_like(value)) for h in range(heads)], axis=1
            )
        )

    passed = slabs * (quad - 1)
    drain(b_recv.at[pl.ds(0, passed), :, pl.ds(0, b_used)], b_recv_sem.at[0])
    b_rows = b_recv.shape[2]
    gathered = b_recv.reshape(n * groups * b_rows, 128)
    for h in range(heads):
        for a in range(rows):
            first_row = h // own_heads * b_rows + h % own_heads * rows + a
            bias[pl.ds(h * width + a, n, rows), :] = gathered[
                pl.ds(first_row, n, groups * b_rows), :
            ]

    scale = 1.0 / math.sqrt(size)
    blank = jnp.zeros((128 - width, 128), BF16)
    for c in range(cols):
        weights, inverse = [], []
        for h in range(heads):
            part = slice(h * width, (h + 1) * width)
            score = scores[c][part] * scale + bias[part, :]
            exponent = jnp.exp(score - jnp.max(score, axis=0, keepdims=True))
            total = jnp.sum(exponent, axis=0, keepdims=True)
            weights += [exponent.astype(BF16), blank]
            inverse.append(jnp.broadcast_to(1.0 / total, (size, 128)))
        attended = jnp.dot(values[c], jnp.concatenate(weights, axis=0), preferred_element_type=F32)
        result = attended * jnp.concatenate(inverse, axis=0) * gating[:, c * 128 : (c + 1) * 128]
        gated[c * 128 : (c + 1) * 128, :] = result.T

    g_rows = g_send.shape[1]
    for i in range(own_rows):
        for c in range(cols):
            g_stage[pl.ds(i * cols + c, devices, g_rows), :] = gated[
                pl.ds(c * 128 + i, devices, own_rows), :
            ]
    g_send[...] = g_stage[...].reshape(devices, g_rows, -1).astype(BF16)

    for offset, plane in sorted(others, key=lambda o: -min(o[0], n - o[0])):
        other_d, other_g = dap_at[offset], planes[plane]
        send(
            g_send.at[other_d * groups + other_g],
            g_recv.at[me],
            g_send_sem,
            g_recv_sem,
            other_d,
            other_g,
        )
    g_recv[me] = g_send[d * groups + g]
    drain(b_recv.at[pl.ds(0, len(first)), 0, pl.ds(0, b_used)], b_send_sem.at[0])
    drain(b_recv.at[pl.ds(0, passed), :, pl.ds(0, b_used)], b_send_sem.at[1])
    drain(x_send.at[pl.ds(0, n - 1)], x_send_sem)
    w_copy.wait_send()
    drain(g_send.at[pl.ds(0, devices - 1)], g_send_sem)
    w_out = jnp.concatenate([w_all[k, low_out : low_out + inner, :] for k in range(groups)], axis=0)
    drain(g_recv.at[pl.ds(0, devices - 1)], g_recv_sem)
    projected[...] = jnp.dot(
        g_recv[...].reshape(devices * g_rows, -1), w_out, preferred_element_type=F32
    )
    for i in range(own_rows):
        for c in range(cols):
            out_ref[i, c * devices : (c + 1) * devices, :] = projected[
                pl.ds(i * cols + c, devices, g_rows), :
            ].astype(BF16)


def fused(n, groups, pair, ln_gain, ln_shift, w_project, w_bias, w_out):
    rows, width, channels = pair.shape
    own_heads = w_bias.shape[1]
    heads = own_heads * groups
    size = w_project.shape[2] // own_heads
    devices = n * groups
    cols = width // devices
    own_rows = rows // groups
    inner = own_heads * size
    w_rows = 5 * inner
    b_rows = up(own_heads * rows, 8)
    x_rows = up(rows * cols, 16)
    g_rows = up(own_rows * cols, 16)
    dims = (n, groups, rows, width, cols, heads, size)
    vmem = pl.BlockSpec(memory_space=pltpu.VMEM)
    hbm = pl.BlockSpec(memory_space=pl.ANY)
    sems = pltpu.SemaphoreType.DMA
    return pl.pallas_call(
        functools.partial(kernel, dims),
        out_shape=pltpu.VMEM((own_rows, width, channels), BF16),
        in_specs=[hbm] * 6,
        out_specs=vmem,
        scratch_shapes=[
            pltpu.VMEM((rows, width, channels), BF16),
            pltpu.VMEM((1, channels), F32),
            pltpu.VMEM((1, channels), F32),
            pltpu.VMEM((own_heads, channels), BF16),
            pltpu.VMEM((rows * 128, channels), F32),
            pltpu.VMEM((n * x_rows, channels), F32),
            pltpu.VMEM((n, x_rows, channels), BF16),
            pltpu.VMEM((n, x_rows, channels), BF16),
            pltpu.VMEM((cols * 128, channels), F32),
            pltpu.VMEM((groups, w_rows, channels), BF16),
            pltpu.VMEM((16, channels), BF16),
            pltpu.VMEM((n, groups, b_rows, 128), F32),
            pltpu.VMEM((heads * width, 128), F32),
            pltpu.VMEM((cols * 128, heads * size), F32),
            pltpu.VMEM((devices * g_rows, heads * size), F32),
            pltpu.VMEM((devices, g_rows, heads * size), BF16),
            pltpu.VMEM((devices, g_rows, heads * size), BF16),
            pltpu.VMEM((devices * g_rows, channels), F32),
            sems((6,)),
            sems(()),
            sems(()),
            sems(()),
            sems(()),
            sems((2,)),
            sems((n // min(4, n) * groups,)),
            sems(()),
            sems(()),
        ],
        compiler_params=pltpu.CompilerParams(
            collective_id=0, has_side_effects=True, vmem_limit_bytes=VMEM_BYTES
        ),
    )(
        pair,
        ln_gain.reshape(1, -1),
        ln_shift.reshape(1, -1),
        w_bias.T,
        jnp.transpose(w_project, (1, 2, 0)).reshape(-1, channels),
        w_out,
    )


def normalize(pair, ln_gain, ln_shift):
    values_f = pair.astype(jnp.float32)
    average = jnp.mean(values_f, axis=-1, keepdims=True)
    centred = values_f - average
    variance = jnp.mean(centred * centred, axis=-1, keepdims=True)
    return (centred * lax.rsqrt(variance + 1e-05) * ln_gain + ln_shift).astype(jnp.bfloat16)


def project_entries(normed, flat_w):
    projected = jnp.dot(normed, flat_w, preferred_element_type=jnp.float32)
    head_width = flat_w.shape[1] // 4
    head_part = projected[..., : 3 * head_width].astype(jnp.bfloat16)
    gating = jax.nn.sigmoid(projected[..., 3 * head_width :]).astype(jnp.bfloat16)
    return jnp.concatenate([head_part, gating], axis=-1)


def local(pair, ln_gain, ln_shift, w_project, w_bias, w_out):
    row_count, width_n, channels = pair.shape
    heads_here = w_bias.shape[1]
    head_size = w_project.shape[2] // heads_here
    flat_w = w_project.reshape(channels, -1)
    normed_rows = normalize(pair, ln_gain, ln_shift)
    bias_rows = jnp.einsum("abc,ch->hab", normed_rows, w_bias, preferred_element_type=jnp.float32)
    bias_all = lax.all_gather(bias_rows, "dap", axis=1, tiled=True)
    bias_key_last = jnp.swapaxes(bias_all, 1, 2)
    dap_count = lax.axis_size("dap")
    blocks = pair.reshape(row_count, dap_count, width_n // dap_count, channels)
    packed = project_entries(
        normalize(
            lax.all_to_all(blocks, "dap", split_axis=1, concat_axis=0, tiled=True),
            ln_gain,
            ln_shift,
        ),
        flat_w,
    )
    packed = packed.reshape(width_n, row_count, -1)

    def attend(index):
        column_data = lax.dynamic_index_in_dim(packed, index, 1, keepdims=False)
        pieces = column_data.reshape(width_n, 4, heads_here, head_size)
        scores = jnp.einsum(
            "ihc,khc->hik", pieces[:, 0], pieces[:, 1], preferred_element_type=jnp.float32
        )
        scores = scores * (1.0 / math.sqrt(head_size)) + bias_key_last
        highest = jnp.max(scores, axis=-1, keepdims=True)
        exponent = jnp.exp(scores - highest)
        totals = jnp.sum(exponent, axis=-1)
        weights = exponent.astype(jnp.bfloat16)
        attended = jnp.einsum(
            "hik,khc->ihc", weights, pieces[:, 2], preferred_element_type=jnp.float32
        )
        attended = attended / jnp.swapaxes(totals, 0, 1)[..., None]
        gated_out = (attended * pieces[:, 3].astype(jnp.float32)).astype(jnp.bfloat16)
        return gated_out.reshape(width_n, heads_here * head_size)

    gated_cols = lax.map(attend, jnp.arange(row_count, dtype=jnp.int32))
    returned = lax.all_to_all(
        gated_cols.reshape(row_count, -1), "dap", split_axis=1, concat_axis=0, tiled=True
    )
    returned = returned.reshape(width_n, row_count, heads_here * head_size)
    update = lax.psum_scatter(
        jnp.einsum("jic,cd->ijd", returned, w_out, preferred_element_type=jnp.float32),
        "heads",
        scatter_dimension=0,
        tiled=True,
    )
    return update.astype(jnp.bfloat16)


def fits(mesh, pair, w_project, w_bias):
    n, groups = mesh.shape["dap"], mesh.shape["heads"]
    rows, width, channels = pair.shape
    devices = n * groups
    heads = w_bias.shape[1] * groups
    return (
        groups == 2
        and channels == 128
        and width <= 128
        and width % devices == 0
        and width % 32 == 0
        and w_project.shape[2] * groups == 128
        and n % 8 == 0
        and rows % groups == 0
    )


def solution(mesh):
    n, groups = mesh.shape["dap"], mesh.shape["heads"]

    def run(pair, ln_gain, ln_shift, w_project, w_bias, w_out):
        if fits(mesh, pair, w_project, w_bias):
            return fused(n, groups, pair, ln_gain, ln_shift, w_project, w_bias, w_out)
        return local(pair, ln_gain, ln_shift, w_project, w_bias, w_out)

    in_specs = (
        P("dap", None, None),
        P(),
        P(),
        P(None, None, "heads"),
        P(None, "heads"),
        P("heads", None),
    )
    out_specs = P(("dap", "heads"), None, None)
    return jax.shard_map(run, mesh=mesh, in_specs=in_specs, out_specs=out_specs, check_vma=False)
```

```python
import functools
import math

import jax
import jax.numpy as jnp
from jax import lax
from jax.experimental import pallas as pl
from jax.experimental.pallas import tpu as pltpu
from jax.sharding import PartitionSpec as P

MESH = pl.DeviceIdType.MESH
F32 = jnp.float32
BF16 = jnp.bfloat16
NT = (((1,), (1,)), ((), ()))
VMEM_BYTES = 60 * 1024 * 1024


def up(size, unit):
    return -(-size // unit) * unit


def nt_dot(left, right):
    return lax.dot_general(left, right, NT, preferred_element_type=F32)


def kernel(
    dims,
    pair_hbm,
    gain_hbm,
    shift_hbm,
    bias_hbm,
    project_hbm,
    w_out_hbm,
    out_ref,
    pair_ref,
    gain_ref,
    shift_ref,
    bias_ref,
    normed,
    stage,
    x_send,
    x_recv,
    tokens,
    w_all,
    b_pad,
    b_recv,
    bias,
    gated,
    g_stage,
    g_send,
    g_recv,
    projected,
    load_sem,
    w_send_sem,
    w_recv_sem,
    x_send_sem,
    x_recv_sem,
    b_send_sem,
    b_recv_sem,
    g_send_sem,
    g_recv_sem,
):
    n, groups, rows, width, cols, heads, size = dims
    own_heads = heads // groups
    inner = own_heads * size
    devices = n * groups
    own_rows = rows // groups
    d = lax.axis_index("dap")
    g = lax.axis_index("heads")
    me = g * n + d
    quad = 4
    slabs = n // quad
    z, r = d // quad, lax.rem(d, quad)
    planes = [g, 1 - g]
    dap_at = [lax.rem(d + offset, n) for offset in range(n)]
    slab_at = [lax.rem(z + back, slabs) * quad for back in range(slabs)]
    near_at = [lax.rem(r + near, quad) for near in range(quad)]

    low_out = 4 * inner
    loads = [
        pltpu.make_async_copy(pair_hbm, pair_ref, load_sem.at[0]),
        pltpu.make_async_copy(gain_hbm, gain_ref, load_sem.at[4]),
        pltpu.make_async_copy(shift_hbm, shift_ref, load_sem.at[5]),
    ]
    w_loads = [
        pltpu.make_async_copy(bias_hbm, bias_ref, load_sem.at[1]),
        pltpu.make_async_copy(project_hbm, w_all.at[g, pl.ds(0, low_out)], load_sem.at[2]),
        pltpu.make_async_copy(w_out_hbm, w_all.at[g, pl.ds(low_out, inner)], load_sem.at[3]),
    ]
    for copy in loads + w_loads:
        copy.start()

    barrier = pltpu.get_barrier_semaphore()
    others = [(k % n, k // n) for k in range(1, devices)]
    for offset, plane in others:
        pl.semaphore_signal(
            barrier, inc=1, device_id=(dap_at[offset], planes[plane]), device_id_type=MESH
        )

    for copy in loads:
        copy.wait()
    gain = gain_ref[...]
    shift = shift_ref[...]
    for a in range(rows):
        values = pair_ref[a].astype(F32)
        average = jnp.mean(values, axis=-1, keepdims=True)
        centred = values - average
        variance = jnp.mean(centred * centred, axis=-1, keepdims=True)
        normed[a * 128 : a * 128 + width, :] = (
            centred * lax.rsqrt(variance + 1e-05) * gain + shift
        )

    x_rows = x_send.shape[1]
    for a in range(rows):
        for c in range(cols):
            start = pl.multiple_of(a * 128 + c * devices + g * n, 8)
            stage[pl.ds(a * cols + c, n, x_rows), :] = normed[pl.ds(start, n), :]
    x_send[...] = stage[...].reshape(n, x_rows, -1).astype(BF16)

    w_loads[0].wait()
    b_pad[0:own_heads, :] = bias_ref[...]
    w_bias = b_pad[...]
    part = nt_dot(w_bias, normed[...].astype(BF16))
    for a in range(rows):
        for h in range(own_heads):
            row = h * rows + a
            b_recv[z, r, g, row : row + 1, :] = part[h : h + 1, a * 128 : (a + 1) * 128]
    for c in range(cols):
        tokens[c * 128 + width : (c + 1) * 128, :] = jnp.zeros((128 - width, 128), F32)
    for copy in w_loads[1:]:
        copy.wait()

    pl.semaphore_wait(barrier, devices - 1)

    def send(src, dst, send_sem, recv_sem, other, plane=g):
        copy = pltpu.make_async_remote_copy(
            src_ref=src,
            dst_ref=dst,
            send_sem=send_sem,
            recv_sem=recv_sem,
            device_id=(other, plane),
            device_id_type=MESH,
        )
        copy.start()
        return copy

    def drain(ref, sem):
        pltpu.make_async_copy(ref, ref, sem).wait()

    b_used = own_heads * rows
    own_bias = b_recv.at[z, r, g, pl.ds(0, b_used)]
    first = [(back, plane) for plane in range(groups) for back in range(slabs)][1:]
    across = {}
    for back, plane in first:
        k = back * groups + plane
        across[back, plane] = send(
            own_bias, own_bias, b_send_sem.at[k], b_recv_sem.at[k], slab_at[back] + r, planes[plane]
        )

    far = [near + back * quad for back in range(1, slabs) for near in range(quad)]
    for offset in far + list(range(1, quad)):
        other = slab_at[offset // quad] + near_at[offset % quad]
        send(x_send.at[other], x_recv.at[d], x_send_sem, x_recv_sem, other)
    own_w = w_all.at[g]
    w_copy = send(own_w, own_w, w_send_sem, w_recv_sem, d, planes[1])
    x_recv[d] = x_send[d]

    def pass_on(place, other, k):
        column = b_recv.at[:, place, :, pl.ds(0, b_used)]
        return send(column, column, b_send_sem.at[k], b_recv_sem.at[k], z * quad + other)

    for copy in across.values():
        copy.wait_recv()
    r_y = lax.rem(r + 2, quad)
    r_core = r + 1 - 2 * lax.rem(r, 2)
    hop = slabs * groups
    y_copy = pass_on(r, r_y, hop)
    core_copies = [pass_on(r, r_core, hop + 1)]

    drain(x_recv.at[pl.ds(0, n - 1)], x_recv_sem)
    stage[...] = x_recv[...].reshape(n * x_rows, -1).astype(F32)
    for a in range(rows):
        for c in range(cols):
            tokens[pl.ds(c * 128 + a, n, rows), :] = stage[pl.ds(a * cols + c, n, x_rows), :]
    entries = tokens[...].astype(BF16)

    w_copy.wait_recv()

    def weight(t):
        low = t * inner
        return jnp.concatenate([w_all[k, low : low + inner, :] for k in range(groups)], axis=0)

    keys = nt_dot(entries, weight(1)).astype(BF16)
    channels = heads * size
    w_rest = jnp.concatenate([weight(0), weight(2), weight(3)], axis=0)
    rest = nt_dot(w_rest, entries)
    queries = rest[:channels].astype(BF16)
    all_values = rest[channels : 2 * channels].astype(BF16)
    gating = jax.nn.sigmoid(rest[2 * channels :]).astype(BF16).astype(F32)
    lane = lax.broadcasted_iota(jnp.int32, (width, channels), 1) // size
    row = lax.broadcasted_iota(jnp.int32, (channels, 128), 0) // size
    scores, values = [], []
    for c in range(cols):
        key = keys[c * 128 : c * 128 + width]
        stacked = jnp.concatenate(
            [jnp.where(lane == h, key, jnp.zeros_like(key)) for h in range(heads)], axis=0
        )
        part = slice(c * 128, (c + 1) * 128)
        scores.append(jnp.dot(stacked, queries[:, part], preferred_element_type=F32))
        value = all_values[:, part]
        values.append(
            jnp.concatenate(
                [jnp.where(row == h, value, jnp.zeros_like(value)) for h in range(heads)], axis=1
            )
        )

    y_copy.wait_recv()
    core_copies.append(pass_on(r_y, r_core, hop + 2))
    for copy in core_copies:
        copy.wait_recv()
    b_rows = b_recv.shape[3]
    gathered = b_recv.reshape(n * groups * b_rows, 128)
    for h in range(heads):
        for a in range(rows):
            first_row = h // own_heads * b_rows + h % own_heads * rows + a
            bias[pl.ds(h * width + a, n, rows), :] = gathered[
                pl.ds(first_row, n, groups * b_rows), :
            ]

    scale = 1.0 / math.sqrt(size)
    blank = jnp.zeros((128 - width, 128), BF16)
    for c in range(cols):
        weights, inverse = [], []
        for h in range(heads):
            part = slice(h * width, (h + 1) * width)
            score = scores[c][part] * scale + bias[part, :]
            exponent = jnp.exp(score - jnp.max(score, axis=0, keepdims=True))
            total = jnp.sum(exponent, axis=0, keepdims=True)
            weights += [exponent.astype(BF16), blank]
            inverse.append(jnp.broadcast_to(1.0 / total, (size, 128)))
        attended = jnp.dot(values[c], jnp.concatenate(weights, axis=0), preferred_element_type=F32)
        result = attended * jnp.concatenate(inverse, axis=0) * gating[:, c * 128 : (c + 1) * 128]
        gated[c * 128 : (c + 1) * 128, :] = result.T

    g_rows = g_send.shape[1]
    for i in range(own_rows):
        for c in range(cols):
            g_stage[pl.ds(i * cols + c, devices, g_rows), :] = gated[
                pl.ds(c * 128 + i, devices, own_rows), :
            ]
    g_send[...] = g_stage[...].reshape(devices, g_rows, -1).astype(BF16)

    for offset, plane in sorted(others, key=lambda o: -min(o[0], n - o[0])):
        other_d, other_g = dap_at[offset], planes[plane]
        send(
            g_send.at[other_d * groups + other_g],
            g_recv.at[me],
            g_send_sem,
            g_recv_sem,
            other_d,
            other_g,
        )
    g_recv[me] = g_send[d * groups + g]
    for copy in [*across.values(), y_copy, *core_copies]:
        copy.wait_send()
    drain(x_send.at[pl.ds(0, n - 1)], x_send_sem)
    w_copy.wait_send()
    drain(g_send.at[pl.ds(0, devices - 1)], g_send_sem)
    w_out = jnp.concatenate([w_all[k, low_out : low_out + inner, :] for k in range(groups)], axis=0)
    drain(g_recv.at[pl.ds(0, devices - 1)], g_recv_sem)
    projected[...] = jnp.dot(
        g_recv[...].reshape(devices * g_rows, -1), w_out, preferred_element_type=F32
    )
    for i in range(own_rows):
        for c in range(cols):
            out_ref[i, c * devices : (c + 1) * devices, :] = projected[
                pl.ds(i * cols + c, devices, g_rows), :
            ].astype(BF16)


def fused(n, groups, pair, ln_gain, ln_shift, w_project, w_bias, w_out):
    rows, width, channels = pair.shape
    own_heads = w_bias.shape[1]
    heads = own_heads * groups
    size = w_project.shape[2] // own_heads
    devices = n * groups
    cols = width // devices
    own_rows = rows // groups
    inner = own_heads * size
    w_rows = 5 * inner
    b_rows = up(own_heads * rows, 8)
    x_rows = up(rows * cols, 16)
    g_rows = up(own_rows * cols, 16)
    dims = (n, groups, rows, width, cols, heads, size)
    vmem = pl.BlockSpec(memory_space=pltpu.VMEM)
    hbm = pl.BlockSpec(memory_space=pl.ANY)
    sems = pltpu.SemaphoreType.DMA
    return pl.pallas_call(
        functools.partial(kernel, dims),
        out_shape=pltpu.VMEM((own_rows, width, channels), BF16),
        in_specs=[hbm] * 6,
        out_specs=vmem,
        scratch_shapes=[
            pltpu.VMEM((rows, width, channels), BF16),
            pltpu.VMEM((1, channels), F32),
            pltpu.VMEM((1, channels), F32),
            pltpu.VMEM((own_heads, channels), BF16),
            pltpu.VMEM((rows * 128, channels), F32),
            pltpu.VMEM((n * x_rows, channels), F32),
            pltpu.VMEM((n, x_rows, channels), BF16),
            pltpu.VMEM((n, x_rows, channels), BF16),
            pltpu.VMEM((cols * 128, channels), F32),
            pltpu.VMEM((groups, w_rows, channels), BF16),
            pltpu.VMEM((16, channels), BF16),
            pltpu.VMEM((n // 4, 4, groups, b_rows, 128), F32),
            pltpu.VMEM((heads * width, 128), F32),
            pltpu.VMEM((cols * 128, heads * size), F32),
            pltpu.VMEM((devices * g_rows, heads * size), F32),
            pltpu.VMEM((devices, g_rows, heads * size), BF16),
            pltpu.VMEM((devices, g_rows, heads * size), BF16),
            pltpu.VMEM((devices * g_rows, channels), F32),
            sems((6,)),
            sems(()),
            sems(()),
            sems(()),
            sems(()),
            sems((n // 4 * groups + 3,)),
            sems((n // 4 * groups + 3,)),
            sems(()),
            sems(()),
        ],
        compiler_params=pltpu.CompilerParams(
            collective_id=0, has_side_effects=True, vmem_limit_bytes=VMEM_BYTES
        ),
    )(
        pair,
        ln_gain.reshape(1, -1),
        ln_shift.reshape(1, -1),
        w_bias.T,
        jnp.transpose(w_project, (1, 2, 0)).reshape(-1, channels),
        w_out,
    )


def normalize(pair, ln_gain, ln_shift):
    values_f = pair.astype(jnp.float32)
    average = jnp.mean(values_f, axis=-1, keepdims=True)
    centred = values_f - average
    variance = jnp.mean(centred * centred, axis=-1, keepdims=True)
    return (centred * lax.rsqrt(variance + 1e-05) * ln_gain + ln_shift).astype(jnp.bfloat16)


def project_entries(normed, flat_w):
    projected = jnp.dot(normed, flat_w, preferred_element_type=jnp.float32)
    head_width = flat_w.shape[1] // 4
    head_part = projected[..., : 3 * head_width].astype(jnp.bfloat16)
    gating = jax.nn.sigmoid(projected[..., 3 * head_width :]).astype(jnp.bfloat16)
    return jnp.concatenate([head_part, gating], axis=-1)


def local(pair, ln_gain, ln_shift, w_project, w_bias, w_out):
    row_count, width_n, channels = pair.shape
    heads_here = w_bias.shape[1]
    head_size = w_project.shape[2] // heads_here
    flat_w = w_project.reshape(channels, -1)
    normed_rows = normalize(pair, ln_gain, ln_shift)
    bias_rows = jnp.einsum("abc,ch->hab", normed_rows, w_bias, preferred_element_type=jnp.float32)
    bias_all = lax.all_gather(bias_rows, "dap", axis=1, tiled=True)
    bias_key_last = jnp.swapaxes(bias_all, 1, 2)
    dap_count = lax.axis_size("dap")
    blocks = pair.reshape(row_count, dap_count, width_n // dap_count, channels)
    packed = project_entries(
        normalize(
            lax.all_to_all(blocks, "dap", split_axis=1, concat_axis=0, tiled=True),
            ln_gain,
            ln_shift,
        ),
        flat_w,
    )
    packed = packed.reshape(width_n, row_count, -1)

    def attend(index):
        column_data = lax.dynamic_index_in_dim(packed, index, 1, keepdims=False)
        pieces = column_data.reshape(width_n, 4, heads_here, head_size)
        scores = jnp.einsum(
            "ihc,khc->hik", pieces[:, 0], pieces[:, 1], preferred_element_type=jnp.float32
        )
        scores = scores * (1.0 / math.sqrt(head_size)) + bias_key_last
        highest = jnp.max(scores, axis=-1, keepdims=True)
        exponent = jnp.exp(scores - highest)
        totals = jnp.sum(exponent, axis=-1)
        weights = exponent.astype(jnp.bfloat16)
        attended = jnp.einsum(
            "hik,khc->ihc", weights, pieces[:, 2], preferred_element_type=jnp.float32
        )
        attended = attended / jnp.swapaxes(totals, 0, 1)[..., None]
        gated_out = (attended * pieces[:, 3].astype(jnp.float32)).astype(jnp.bfloat16)
        return gated_out.reshape(width_n, heads_here * head_size)

    gated_cols = lax.map(attend, jnp.arange(row_count, dtype=jnp.int32))
    returned = lax.all_to_all(
        gated_cols.reshape(row_count, -1), "dap", split_axis=1, concat_axis=0, tiled=True
    )
    returned = returned.reshape(width_n, row_count, heads_here * head_size)
    update = lax.psum_scatter(
        jnp.einsum("jic,cd->ijd", returned, w_out, preferred_element_type=jnp.float32),
        "heads",
        scatter_dimension=0,
        tiled=True,
    )
    return update.astype(jnp.bfloat16)


def fits(mesh, pair, w_project, w_bias):
    n, groups = mesh.shape["dap"], mesh.shape["heads"]
    rows, width, channels = pair.shape
    devices = n * groups
    heads = w_bias.shape[1] * groups
    return (
        groups == 2
        and channels == 128
        and width <= 128
        and width % devices == 0
        and width % 32 == 0
        and w_project.shape[2] * groups == 128
        and n % 8 == 0
        and rows % groups == 0
    )


def solution(mesh):
    n, groups = mesh.shape["dap"], mesh.shape["heads"]

    def run(pair, ln_gain, ln_shift, w_project, w_bias, w_out):
        if fits(mesh, pair, w_project, w_bias):
            return fused(n, groups, pair, ln_gain, ln_shift, w_project, w_bias, w_out)
        return local(pair, ln_gain, ln_shift, w_project, w_bias, w_out)

    in_specs = (
        P("dap", None, None),
        P(),
        P(),
        P(None, None, "heads"),
        P(None, "heads"),
        P("heads", None),
    )
    out_specs = P(("dap", "heads"), None, None)
    return jax.shard_map(run, mesh=mesh, in_specs=in_specs, out_specs=out_specs, check_vma=False)
```

```python
import functools
import math

import jax
import jax.numpy as jnp
from jax import lax
from jax.experimental import pallas as pl
from jax.experimental.pallas import tpu as pltpu
from jax.sharding import PartitionSpec as P

MESH = pl.DeviceIdType.MESH
F32 = jnp.float32
BF16 = jnp.bfloat16
NT = (((1,), (1,)), ((), ()))
VMEM_BYTES = 60 * 1024 * 1024


def up(size, unit):
    return -(-size // unit) * unit


def nt_dot(left, right):
    return lax.dot_general(left, right, NT, preferred_element_type=F32)


def kernel(
    dims,
    pair_hbm,
    gain_hbm,
    shift_hbm,
    bias_hbm,
    project_hbm,
    w_out_hbm,
    out_ref,
    pair_ref,
    gain_ref,
    shift_ref,
    bias_ref,
    normed,
    stage,
    x_send,
    x_recv,
    tokens,
    w_all,
    b_pad,
    b_recv,
    bias,
    gated,
    g_stage,
    g_send,
    g_recv,
    projected,
    load_sem,
    w_send_sem,
    w_recv_sem,
    x_send_sem,
    x_recv_sem,
    b_send_sem,
    b_recv_sem,
    g_send_sem,
    g_recv_sem,
):
    n, groups, rows, width, cols, heads, size = dims
    own_heads = heads // groups
    inner = own_heads * size
    devices = n * groups
    own_rows = rows // groups
    d = lax.axis_index("dap")
    g = lax.axis_index("heads")
    me = g * n + d
    quad = min(4, n)
    slabs = n // quad
    z, r = d // quad, lax.rem(d, quad)
    planes = [g, 1 - g]
    dap_at = [lax.rem(d + offset, n) for offset in range(n)]
    slab_at = [lax.rem(z + back, slabs) * quad for back in range(slabs)]
    near_at = [lax.rem(r + near, quad) for near in range(quad)]

    low_out = 4 * inner
    loads = [
        pltpu.make_async_copy(pair_hbm, pair_ref, load_sem.at[0]),
        pltpu.make_async_copy(gain_hbm, gain_ref, load_sem.at[4]),
        pltpu.make_async_copy(shift_hbm, shift_ref, load_sem.at[5]),
    ]
    w_loads = [
        pltpu.make_async_copy(bias_hbm, bias_ref, load_sem.at[1]),
        pltpu.make_async_copy(project_hbm, w_all.at[g, pl.ds(0, low_out)], load_sem.at[2]),
        pltpu.make_async_copy(w_out_hbm, w_all.at[g, pl.ds(low_out, inner)], load_sem.at[3]),
    ]
    for copy in loads + w_loads:
        copy.start()

    barrier = pltpu.get_barrier_semaphore()
    others = [(k % n, k // n) for k in range(1, devices)]
    for offset, plane in others:
        pl.semaphore_signal(
            barrier, inc=1, device_id=(dap_at[offset], planes[plane]), device_id_type=MESH
        )

    for copy in loads:
        copy.wait()
    gain = gain_ref[...]
    shift = shift_ref[...]
    for a in range(rows):
        values = pair_ref[a].astype(F32)
        average = jnp.mean(values, axis=-1, keepdims=True)
        centred = values - average
        variance = jnp.mean(centred * centred, axis=-1, keepdims=True)
        normed[a * 128 : a * 128 + width, :] = (
            centred * lax.rsqrt(variance + 1e-05) * gain + shift
        )

    w_loads[0].wait()
    b_pad[0:own_heads, :] = bias_ref[...]
    w_bias = b_pad[...]
    part = nt_dot(w_bias, normed[...].astype(BF16))
    for a in range(rows):
        for h in range(own_heads):
            row = h * rows + a
            b_recv[d, g, row : row + 1, :] = part[h : h + 1, a * 128 : (a + 1) * 128]
    pl.semaphore_wait(barrier, devices - 1)

    def send(src, dst, send_sem, recv_sem, other, plane=g):
        copy = pltpu.make_async_remote_copy(
            src_ref=src,
            dst_ref=dst,
            send_sem=send_sem,
            recv_sem=recv_sem,
            device_id=(other, plane),
            device_id_type=MESH,
        )
        copy.start()
        return copy

    def drain(ref, sem):
        pltpu.make_async_copy(ref, ref, sem).wait()

    b_used = own_heads * rows
    own_bias = b_recv.at[d, g, pl.ds(0, b_used)]
    first = [(back, plane) for plane in range(groups) for back in range(slabs)][1:]
    across = {}
    for back, plane in first:
        k = back * groups + plane
        across[back, plane] = send(
            own_bias, own_bias, b_send_sem.at[0], b_recv_sem.at[k], slab_at[back] + r, planes[plane]
        )

    x_rows = x_send.shape[1]
    for a in range(rows):
        for c in range(cols):
            start = pl.multiple_of(a * 128 + c * devices + g * n, 8)
            stage[pl.ds(a * cols + c, n, x_rows), :] = normed[pl.ds(start, n), :]
    x_send[...] = stage[...].reshape(n, x_rows, -1).astype(BF16)

    far = [near + back * quad for back in range(1, slabs) for near in range(quad)]
    for offset in far + list(range(1, quad)):
        other = slab_at[offset // quad] + near_at[offset % quad]
        send(x_send.at[other], x_recv.at[d], x_send_sem, x_recv_sem, other)
    for copy in w_loads[1:]:
        copy.wait()
    own_w = w_all.at[g]
    w_copy = send(own_w, own_w, w_send_sem, w_recv_sem, d, planes[1])
    x_recv[d] = x_send[d]

    for c in range(cols):
        tokens[c * 128 + width : (c + 1) * 128, :] = jnp.zeros((128 - width, 128), F32)

    for back in range(slabs):
        for plane in range(groups):
            if back or plane:
                across[back, plane].wait_recv()
        block = slab_at[(slabs - back) % slabs] + r
        both = b_recv.at[block, :, pl.ds(0, b_used)]
        for near in range(1, quad):
            send(both, both, b_send_sem.at[1], b_recv_sem.at[0], slab_at[0] + near_at[near])

    drain(x_recv.at[pl.ds(0, n - 1)], x_recv_sem)
    stage[...] = x_recv[...].reshape(n * x_rows, -1).astype(F32)
    for a in range(rows):
        for c in range(cols):
            tokens[pl.ds(c * 128 + a, n, rows), :] = stage[pl.ds(a * cols + c, n, x_rows), :]
    entries = tokens[...].astype(BF16)

    w_copy.wait_recv()

    def weight(t):
        low = t * inner
        return jnp.concatenate([w_all[k, low : low + inner, :] for k in range(groups)], axis=0)

    keys = nt_dot(entries, weight(1)).astype(BF16)
    channels = heads * size
    w_rest = jnp.concatenate([weight(0), weight(2), weight(3)], axis=0)
    rest = nt_dot(w_rest, entries)
    queries = rest[:channels].astype(BF16)
    all_values = rest[channels : 2 * channels].astype(BF16)
    gating = jax.nn.sigmoid(rest[2 * channels :]).astype(BF16).astype(F32)
    lane = lax.broadcasted_iota(jnp.int32, (width, channels), 1) // size
    row = lax.broadcasted_iota(jnp.int32, (channels, 128), 0) // size
    scores, values = [], []
    for c in range(cols):
        key = keys[c * 128 : c * 128 + width]
        stacked = jnp.concatenate(
            [jnp.where(lane == h, key, jnp.zeros_like(key)) for h in range(heads)], axis=0
        )
        part = slice(c * 128, (c + 1) * 128)
        scores.append(jnp.dot(stacked, queries[:, part], preferred_element_type=F32))
        value = all_values[:, part]
        values.append(
            jnp.concatenate(
                [jnp.where(row == h, value, jnp.zeros_like(value)) for h in range(heads)], axis=1
            )
        )

    passed = slabs * (quad - 1)
    drain(b_recv.at[pl.ds(0, passed), :, pl.ds(0, b_used)], b_recv_sem.at[0])
    b_rows = b_recv.shape[2]
    gathered = b_recv.reshape(n * groups * b_rows, 128)
    for h in range(heads):
        for a in range(rows):
            first_row = h // own_heads * b_rows + h % own_heads * rows + a
            bias[pl.ds(h * width + a, n, rows), :] = gathered[
                pl.ds(first_row, n, groups * b_rows), :
            ]

    scale = 1.0 / math.sqrt(size)
    blank = jnp.zeros((128 - width, 128), BF16)
    for c in range(cols):
        weights, inverse = [], []
        for h in range(heads):
            part = slice(h * width, (h + 1) * width)
            score = scores[c][part] * scale + bias[part, :]
            exponent = jnp.exp(score - jnp.max(score, axis=0, keepdims=True))
            total = jnp.sum(exponent, axis=0, keepdims=True)
            weights += [exponent.astype(BF16), blank]
            inverse.append(jnp.broadcast_to(1.0 / total, (size, 128)))
        attended = jnp.dot(values[c], jnp.concatenate(weights, axis=0), preferred_element_type=F32)
        result = attended * jnp.concatenate(inverse, axis=0) * gating[:, c * 128 : (c + 1) * 128]
        gated[c * 128 : (c + 1) * 128, :] = result.T

    g_rows = g_send.shape[1]
    for i in range(own_rows):
        for c in range(cols):
            g_stage[pl.ds(i * cols + c, devices, g_rows), :] = gated[
                pl.ds(c * 128 + i, devices, own_rows), :
            ]
    g_send[...] = g_stage[...].reshape(devices, g_rows, -1).astype(BF16)

    for offset, plane in sorted(others, key=lambda o: -min(o[0], n - o[0])):
        other_d, other_g = dap_at[offset], planes[plane]
        send(
            g_send.at[other_d * groups + other_g],
            g_recv.at[me],
            g_send_sem,
            g_recv_sem,
            other_d,
            other_g,
        )
    g_recv[me] = g_send[d * groups + g]
    drain(b_recv.at[pl.ds(0, len(first)), 0, pl.ds(0, b_used)], b_send_sem.at[0])
    drain(b_recv.at[pl.ds(0, passed), :, pl.ds(0, b_used)], b_send_sem.at[1])
    drain(x_send.at[pl.ds(0, n - 1)], x_send_sem)
    w_copy.wait_send()
    drain(g_send.at[pl.ds(0, devices - 1)], g_send_sem)
    w_out = jnp.concatenate([w_all[k, low_out : low_out + inner, :] for k in range(groups)], axis=0)
    drain(g_recv.at[pl.ds(0, devices - 1)], g_recv_sem)
    projected[...] = jnp.dot(
        g_recv[...].reshape(devices * g_rows, -1), w_out, preferred_element_type=F32
    )
    for i in range(own_rows):
        for c in range(cols):
            out_ref[i, c * devices : (c + 1) * devices, :] = projected[
                pl.ds(i * cols + c, devices, g_rows), :
            ].astype(BF16)


def fused(n, groups, pair, ln_gain, ln_shift, w_project, w_bias, w_out):
    rows, width, channels = pair.shape
    own_heads = w_bias.shape[1]
    heads = own_heads * groups
    size = w_project.shape[2] // own_heads
    devices = n * groups
    cols = width // devices
    own_rows = rows // groups
    inner = own_heads * size
    w_rows = 5 * inner
    b_rows = up(own_heads * rows, 8)
    x_rows = up(rows * cols, 16)
    g_rows = up(own_rows * cols, 16)
    dims = (n, groups, rows, width, cols, heads, size)
    vmem = pl.BlockSpec(memory_space=pltpu.VMEM)
    hbm = pl.BlockSpec(memory_space=pl.ANY)
    sems = pltpu.SemaphoreType.DMA
    return pl.pallas_call(
        functools.partial(kernel, dims),
        out_shape=pltpu.VMEM((own_rows, width, channels), BF16),
        in_specs=[hbm] * 6,
        out_specs=vmem,
        scratch_shapes=[
            pltpu.VMEM((rows, width, channels), BF16),
            pltpu.VMEM((1, channels), F32),
            pltpu.VMEM((1, channels), F32),
            pltpu.VMEM((own_heads, channels), BF16),
            pltpu.VMEM((rows * 128, channels), F32),
            pltpu.VMEM((n * x_rows, channels), F32),
            pltpu.VMEM((n, x_rows, channels), BF16),
            pltpu.VMEM((n, x_rows, channels), BF16),
            pltpu.VMEM((cols * 128, channels), F32),
            pltpu.VMEM((groups, w_rows, channels), BF16),
            pltpu.VMEM((16, channels), BF16),
            pltpu.VMEM((n, groups, b_rows, 128), F32),
            pltpu.VMEM((heads * width, 128), F32),
            pltpu.VMEM((cols * 128, heads * size), F32),
            pltpu.VMEM((devices * g_rows, heads * size), F32),
            pltpu.VMEM((devices, g_rows, heads * size), BF16),
            pltpu.VMEM((devices, g_rows, heads * size), BF16),
            pltpu.VMEM((devices * g_rows, channels), F32),
            sems((6,)),
            sems(()),
            sems(()),
            sems(()),
            sems(()),
            sems((2,)),
            sems((n // min(4, n) * groups,)),
            sems(()),
            sems(()),
        ],
        compiler_params=pltpu.CompilerParams(
            collective_id=0, has_side_effects=True, vmem_limit_bytes=VMEM_BYTES
        ),
    )(
        pair,
        ln_gain.reshape(1, -1),
        ln_shift.reshape(1, -1),
        w_bias.T,
        jnp.transpose(w_project, (1, 2, 0)).reshape(-1, channels),
        w_out,
    )


def normalize(pair, ln_gain, ln_shift):
    values_f = pair.astype(jnp.float32)
    average = jnp.mean(values_f, axis=-1, keepdims=True)
    centred = values_f - average
    variance = jnp.mean(centred * centred, axis=-1, keepdims=True)
    return (centred * lax.rsqrt(variance + 1e-05) * ln_gain + ln_shift).astype(jnp.bfloat16)


def project_entries(normed, flat_w):
    projected = jnp.dot(normed, flat_w, preferred_element_type=jnp.float32)
    head_width = flat_w.shape[1] // 4
    head_part = projected[..., : 3 * head_width].astype(jnp.bfloat16)
    gating = jax.nn.sigmoid(projected[..., 3 * head_width :]).astype(jnp.bfloat16)
    return jnp.concatenate([head_part, gating], axis=-1)


def local(pair, ln_gain, ln_shift, w_project, w_bias, w_out):
    row_count, width_n, channels = pair.shape
    heads_here = w_bias.shape[1]
    head_size = w_project.shape[2] // heads_here
    flat_w = w_project.reshape(channels, -1)
    normed_rows = normalize(pair, ln_gain, ln_shift)
    bias_rows = jnp.einsum("abc,ch->hab", normed_rows, w_bias, preferred_element_type=jnp.float32)
    bias_all = lax.all_gather(bias_rows, "dap", axis=1, tiled=True)
    bias_key_last = jnp.swapaxes(bias_all, 1, 2)
    dap_count = lax.axis_size("dap")
    blocks = pair.reshape(row_count, dap_count, width_n // dap_count, channels)
    packed = project_entries(
        normalize(
            lax.all_to_all(blocks, "dap", split_axis=1, concat_axis=0, tiled=True),
            ln_gain,
            ln_shift,
        ),
        flat_w,
    )
    packed = packed.reshape(width_n, row_count, -1)

    def attend(index):
        column_data = lax.dynamic_index_in_dim(packed, index, 1, keepdims=False)
        pieces = column_data.reshape(width_n, 4, heads_here, head_size)
        scores = jnp.einsum(
            "ihc,khc->hik", pieces[:, 0], pieces[:, 1], preferred_element_type=jnp.float32
        )
        scores = scores * (1.0 / math.sqrt(head_size)) + bias_key_last
        highest = jnp.max(scores, axis=-1, keepdims=True)
        exponent = jnp.exp(scores - highest)
        totals = jnp.sum(exponent, axis=-1)
        weights = exponent.astype(jnp.bfloat16)
        attended = jnp.einsum(
            "hik,khc->ihc", weights, pieces[:, 2], preferred_element_type=jnp.float32
        )
        attended = attended / jnp.swapaxes(totals, 0, 1)[..., None]
        gated_out = (attended * pieces[:, 3].astype(jnp.float32)).astype(jnp.bfloat16)
        return gated_out.reshape(width_n, heads_here * head_size)

    gated_cols = lax.map(attend, jnp.arange(row_count, dtype=jnp.int32))
    returned = lax.all_to_all(
        gated_cols.reshape(row_count, -1), "dap", split_axis=1, concat_axis=0, tiled=True
    )
    returned = returned.reshape(width_n, row_count, heads_here * head_size)
    update = lax.psum_scatter(
        jnp.einsum("jic,cd->ijd", returned, w_out, preferred_element_type=jnp.float32),
        "heads",
        scatter_dimension=0,
        tiled=True,
    )
    return update.astype(jnp.bfloat16)


def fits(mesh, pair, w_project, w_bias):
    n, groups = mesh.shape["dap"], mesh.shape["heads"]
    rows, width, channels = pair.shape
    devices = n * groups
    heads = w_bias.shape[1] * groups
    return (
        groups == 2
        and channels == 128
        and width <= 128
        and width % devices == 0
        and width % 32 == 0
        and w_project.shape[2] * groups == 128
        and n % 8 == 0
        and rows % groups == 0
    )


def solution(mesh):
    n, groups = mesh.shape["dap"], mesh.shape["heads"]

    def run(pair, ln_gain, ln_shift, w_project, w_bias, w_out):
        if fits(mesh, pair, w_project, w_bias):
            return fused(n, groups, pair, ln_gain, ln_shift, w_project, w_bias, w_out)
        return local(pair, ln_gain, ln_shift, w_project, w_bias, w_out)

    in_specs = (
        P("dap", None, None),
        P(),
        P(),
        P(None, None, "heads"),
        P(None, "heads"),
        P("heads", None),
    )
    out_specs = P(("dap", "heads"), None, None)
    return jax.shard_map(run, mesh=mesh, in_specs=in_specs, out_specs=out_specs, check_vma=False)
```

```python
import functools
import math

import jax
import jax.numpy as jnp
from jax import lax
from jax.experimental import pallas as pl
from jax.experimental.pallas import tpu as pltpu
from jax.sharding import PartitionSpec as P

MESH = pl.DeviceIdType.MESH
F32 = jnp.float32
BF16 = jnp.bfloat16
NT = (((1,), (1,)), ((), ()))
VMEM_BYTES = 60 * 1024 * 1024


def up(size, unit):
    return -(-size // unit) * unit


def nt_dot(left, right):
    return lax.dot_general(left, right, NT, preferred_element_type=F32)


def kernel(
    dims,
    pair_hbm,
    gain_hbm,
    shift_hbm,
    bias_hbm,
    project_hbm,
    w_out_hbm,
    out_ref,
    pair_ref,
    gain_ref,
    shift_ref,
    bias_ref,
    normed,
    stage,
    x_send,
    x_recv,
    tokens,
    w_all,
    b_pad,
    b_recv,
    bias,
    gated,
    g_stage,
    g_send,
    g_recv,
    projected,
    load_sem,
    w_send_sem,
    w_recv_sem,
    x_send_sem,
    x_recv_sem,
    b_send_sem,
    b_recv_sem,
    g_send_sem,
    g_recv_sem,
):
    n, groups, rows, width, cols, heads, size = dims
    own_heads = heads // groups
    inner = own_heads * size
    devices = n * groups
    own_rows = rows // groups
    d = lax.axis_index("dap")
    g = lax.axis_index("heads")
    me = g * n + d
    quad = min(4, n)
    slabs = n // quad
    z, r = d // quad, lax.rem(d, quad)
    planes = [g, 1 - g]
    dap_at = [lax.rem(d + offset, n) for offset in range(n)]
    slab_at = [lax.rem(z + back, slabs) * quad for back in range(slabs)]
    near_at = [lax.rem(r + near, quad) for near in range(quad)]

    low_out = 4 * inner
    loads = [
        pltpu.make_async_copy(pair_hbm, pair_ref, load_sem.at[0]),
        pltpu.make_async_copy(gain_hbm, gain_ref, load_sem.at[4]),
        pltpu.make_async_copy(shift_hbm, shift_ref, load_sem.at[5]),
    ]
    w_loads = [
        pltpu.make_async_copy(bias_hbm, bias_ref, load_sem.at[1]),
        pltpu.make_async_copy(project_hbm, w_all.at[g, pl.ds(0, low_out)], load_sem.at[2]),
        pltpu.make_async_copy(w_out_hbm, w_all.at[g, pl.ds(low_out, inner)], load_sem.at[3]),
    ]
    for copy in loads + w_loads:
        copy.start()

    barrier = pltpu.get_barrier_semaphore()
    others = [(k % n, k // n) for k in range(1, devices)]
    for offset, plane in others:
        pl.semaphore_signal(
            barrier, inc=1, device_id=(dap_at[offset], planes[plane]), device_id_type=MESH
        )

    for copy in loads:
        copy.wait()
    gain = gain_ref[...]
    shift = shift_ref[...]
    for a in range(rows):
        values = pair_ref[a].astype(F32)
        average = jnp.mean(values, axis=-1, keepdims=True)
        centred = values - average
        variance = jnp.mean(centred * centred, axis=-1, keepdims=True)
        normed[a * 128 : a * 128 + width, :] = (
            centred * lax.rsqrt(variance + 1e-05) * gain + shift
        )

    w_loads[0].wait()
    b_pad[0:own_heads, :] = bias_ref[...]
    w_bias = b_pad[...]
    part = nt_dot(w_bias, normed[...].astype(BF16))
    for a in range(rows):
        for h in range(own_heads):
            row = h * rows + a
            b_recv[d, g, row : row + 1, :] = part[h : h + 1, a * 128 : (a + 1) * 128]
    pl.semaphore_wait(barrier, devices - 1)

    def send(src, dst, send_sem, recv_sem, other, plane=g):
        copy = pltpu.make_async_remote_copy(
            src_ref=src,
            dst_ref=dst,
            send_sem=send_sem,
            recv_sem=recv_sem,
            device_id=(other, plane),
            device_id_type=MESH,
        )
        copy.start()
        return copy

    def drain(ref, sem):
        pltpu.make_async_copy(ref, ref, sem).wait()

    b_used = own_heads * rows
    own_bias = b_recv.at[d, g, pl.ds(0, b_used)]
    first = [(back, plane) for plane in range(groups) for back in range(slabs)][1:]
    across = {}
    for back, plane in first:
        k = back * groups + plane
        across[back, plane] = send(
            own_bias, own_bias, b_send_sem.at[0], b_recv_sem.at[k], slab_at[back] + r, planes[plane]
        )

    x_used = x_send.shape[1]
    x_rows = up(x_used, 8)
    for a in range(rows):
        for c in range(cols):
            start = pl.multiple_of(a * 128 + c * devices + g * n, 8)
            stage[pl.ds(a * cols + c, n, x_rows), :] = normed[pl.ds(start, n), :]
    x_send[...] = stage[...].reshape(n, x_rows, -1)[:, :x_used].astype(BF16)

    far = [near + back * quad for back in range(1, slabs) for near in range(quad)]
    for offset in far + list(range(1, quad)):
        other = slab_at[offset // quad] + near_at[offset % quad]
        send(x_send.at[other], x_recv.at[d], x_send_sem, x_recv_sem, other)
    for copy in w_loads[1:]:
        copy.wait()
    own_w = w_all.at[g]
    w_copy = send(own_w, own_w, w_send_sem, w_recv_sem, d, planes[1])
    x_recv[d] = x_send[d]

    for c in range(cols):
        tokens[c * 128 + width : (c + 1) * 128, :] = jnp.zeros((128 - width, 128), F32)

    for back in range(slabs):
        for plane in range(groups):
            if back or plane:
                across[back, plane].wait_recv()
        block = slab_at[(slabs - back) % slabs] + r
        both = b_recv.at[block, :, pl.ds(0, b_used)]
        for near in range(1, quad):
            send(both, both, b_send_sem.at[1], b_recv_sem.at[0], slab_at[0] + near_at[near])

    drain(x_recv.at[pl.ds(0, n - 1)], x_recv_sem)
    for k in range(n):
        stage[k * x_rows : k * x_rows + x_used, :] = x_recv[k].astype(F32)
    for a in range(rows):
        for c in range(cols):
            tokens[pl.ds(c * 128 + a, n, rows), :] = stage[pl.ds(a * cols + c, n, x_rows), :]
    entries = tokens[...].astype(BF16)

    w_copy.wait_recv()

    def weight(t):
        low = t * inner
        return jnp.concatenate([w_all[k, low : low + inner, :] for k in range(groups)], axis=0)

    keys = nt_dot(entries, weight(1)).astype(BF16)
    channels = heads * size
    w_rest = jnp.concatenate([weight(0), weight(2), weight(3)], axis=0)
    rest = nt_dot(w_rest, entries)
    queries = rest[:channels].astype(BF16)
    all_values = rest[channels : 2 * channels].astype(BF16)
    gating = jax.nn.sigmoid(rest[2 * channels :]).astype(BF16).astype(F32)
    lane = lax.broadcasted_iota(jnp.int32, (width, channels), 1) // size
    row = lax.broadcasted_iota(jnp.int32, (channels, 128), 0) // size
    scores, values = [], []
    for c in range(cols):
        key = keys[c * 128 : c * 128 + width]
        stacked = jnp.concatenate(
            [jnp.where(lane == h, key, jnp.zeros_like(key)) for h in range(heads)], axis=0
        )
        part = slice(c * 128, (c + 1) * 128)
        scores.append(jnp.dot(stacked, queries[:, part], preferred_element_type=F32))
        value = all_values[:, part]
        values.append(
            jnp.concatenate(
                [jnp.where(row == h, value, jnp.zeros_like(value)) for h in range(heads)], axis=1
            )
        )

    passed = slabs * (quad - 1)
    drain(b_recv.at[pl.ds(0, passed), :, pl.ds(0, b_used)], b_recv_sem.at[0])
    b_rows = b_recv.shape[2]
    gathered = b_recv.reshape(n * groups * b_rows, 128)
    for h in range(heads):
        for a in range(rows):
            first_row = h // own_heads * b_rows + h % own_heads * rows + a
            bias[pl.ds(h * width + a, n, rows), :] = gathered[
                pl.ds(first_row, n, groups * b_rows), :
            ]

    scale = 1.0 / math.sqrt(size)
    blank = jnp.zeros((128 - width, 128), BF16)
    for c in range(cols):
        weights, inverse = [], []
        for h in range(heads):
            part = slice(h * width, (h + 1) * width)
            score = scores[c][part] * scale + bias[part, :]
            exponent = jnp.exp(score - jnp.max(score, axis=0, keepdims=True))
            total = jnp.sum(exponent, axis=0, keepdims=True)
            weights += [exponent.astype(BF16), blank]
            inverse.append(jnp.broadcast_to(1.0 / total, (size, 128)))
        attended = jnp.dot(values[c], jnp.concatenate(weights, axis=0), preferred_element_type=F32)
        result = attended * jnp.concatenate(inverse, axis=0) * gating[:, c * 128 : (c + 1) * 128]
        gated[c * 128 : (c + 1) * 128, :] = result.T

    g_rows = g_send.shape[1]
    for i in range(own_rows):
        for c in range(cols):
            g_stage[pl.ds(i * cols + c, devices, g_rows), :] = gated[
                pl.ds(c * 128 + i, devices, own_rows), :
            ]
    g_send[...] = g_stage[...].reshape(devices, g_rows, -1).astype(BF16)

    for offset, plane in sorted(others, key=lambda o: -min(o[0], n - o[0])):
        other_d, other_g = dap_at[offset], planes[plane]
        send(
            g_send.at[other_d * groups + other_g],
            g_recv.at[me],
            g_send_sem,
            g_recv_sem,
            other_d,
            other_g,
        )
    g_recv[me] = g_send[d * groups + g]
    drain(b_recv.at[pl.ds(0, len(first)), 0, pl.ds(0, b_used)], b_send_sem.at[0])
    drain(b_recv.at[pl.ds(0, passed), :, pl.ds(0, b_used)], b_send_sem.at[1])
    drain(x_send.at[pl.ds(0, n - 1)], x_send_sem)
    w_copy.wait_send()
    drain(g_send.at[pl.ds(0, devices - 1)], g_send_sem)
    w_out = jnp.concatenate([w_all[k, low_out : low_out + inner, :] for k in range(groups)], axis=0)
    drain(g_recv.at[pl.ds(0, devices - 1)], g_recv_sem)
    projected[...] = jnp.dot(
        g_recv[...].reshape(devices * g_rows, -1), w_out, preferred_element_type=F32
    )
    for i in range(own_rows):
        for c in range(cols):
            out_ref[i, c * devices : (c + 1) * devices, :] = projected[
                pl.ds(i * cols + c, devices, g_rows), :
            ].astype(BF16)


def fused(n, groups, pair, ln_gain, ln_shift, w_project, w_bias, w_out):
    rows, width, channels = pair.shape
    own_heads = w_bias.shape[1]
    heads = own_heads * groups
    size = w_project.shape[2] // own_heads
    devices = n * groups
    cols = width // devices
    own_rows = rows // groups
    inner = own_heads * size
    w_rows = 5 * inner
    b_rows = up(own_heads * rows, 8)
    x_used = up(rows * cols, 2)
    x_rows = up(x_used, 8)
    g_rows = up(own_rows * cols, 16)
    dims = (n, groups, rows, width, cols, heads, size)
    vmem = pl.BlockSpec(memory_space=pltpu.VMEM)
    hbm = pl.BlockSpec(memory_space=pl.ANY)
    sems = pltpu.SemaphoreType.DMA
    return pl.pallas_call(
        functools.partial(kernel, dims),
        out_shape=pltpu.VMEM((own_rows, width, channels), BF16),
        in_specs=[hbm] * 6,
        out_specs=vmem,
        scratch_shapes=[
            pltpu.VMEM((rows, width, channels), BF16),
            pltpu.VMEM((1, channels), F32),
            pltpu.VMEM((1, channels), F32),
            pltpu.VMEM((own_heads, channels), BF16),
            pltpu.VMEM((rows * 128, channels), F32),
            pltpu.VMEM((n * x_rows, channels), F32),
            pltpu.VMEM((n, x_used, channels), BF16),
            pltpu.VMEM((n, x_used, channels), BF16),
            pltpu.VMEM((cols * 128, channels), F32),
            pltpu.VMEM((groups, w_rows, channels), BF16),
            pltpu.VMEM((16, channels), BF16),
            pltpu.VMEM((n, groups, b_rows, 128), F32),
            pltpu.VMEM((heads * width, 128), F32),
            pltpu.VMEM((cols * 128, heads * size), F32),
            pltpu.VMEM((devices * g_rows, heads * size), F32),
            pltpu.VMEM((devices, g_rows, heads * size), BF16),
            pltpu.VMEM((devices, g_rows, heads * size), BF16),
            pltpu.VMEM((devices * g_rows, channels), F32),
            sems((6,)),
            sems(()),
            sems(()),
            sems(()),
            sems(()),
            sems((2,)),
            sems((n // min(4, n) * groups,)),
            sems(()),
            sems(()),
        ],
        compiler_params=pltpu.CompilerParams(
            collective_id=0, has_side_effects=True, vmem_limit_bytes=VMEM_BYTES
        ),
    )(
        pair,
        ln_gain.reshape(1, -1),
        ln_shift.reshape(1, -1),
        w_bias.T,
        jnp.transpose(w_project, (1, 2, 0)).reshape(-1, channels),
        w_out,
    )


def normalize(pair, ln_gain, ln_shift):
    values_f = pair.astype(jnp.float32)
    average = jnp.mean(values_f, axis=-1, keepdims=True)
    centred = values_f - average
    variance = jnp.mean(centred * centred, axis=-1, keepdims=True)
    return (centred * lax.rsqrt(variance + 1e-05) * ln_gain + ln_shift).astype(jnp.bfloat16)


def project_entries(normed, flat_w):
    projected = jnp.dot(normed, flat_w, preferred_element_type=jnp.float32)
    head_width = flat_w.shape[1] // 4
    head_part = projected[..., : 3 * head_width].astype(jnp.bfloat16)
    gating = jax.nn.sigmoid(projected[..., 3 * head_width :]).astype(jnp.bfloat16)
    return jnp.concatenate([head_part, gating], axis=-1)


def local(pair, ln_gain, ln_shift, w_project, w_bias, w_out):
    row_count, width_n, channels = pair.shape
    heads_here = w_bias.shape[1]
    head_size = w_project.shape[2] // heads_here
    flat_w = w_project.reshape(channels, -1)
    normed_rows = normalize(pair, ln_gain, ln_shift)
    bias_rows = jnp.einsum("abc,ch->hab", normed_rows, w_bias, preferred_element_type=jnp.float32)
    bias_all = lax.all_gather(bias_rows, "dap", axis=1, tiled=True)
    bias_key_last = jnp.swapaxes(bias_all, 1, 2)
    dap_count = lax.axis_size("dap")
    blocks = pair.reshape(row_count, dap_count, width_n // dap_count, channels)
    packed = project_entries(
        normalize(
            lax.all_to_all(blocks, "dap", split_axis=1, concat_axis=0, tiled=True),
            ln_gain,
            ln_shift,
        ),
        flat_w,
    )
    packed = packed.reshape(width_n, row_count, -1)

    def attend(index):
        column_data = lax.dynamic_index_in_dim(packed, index, 1, keepdims=False)
        pieces = column_data.reshape(width_n, 4, heads_here, head_size)
        scores = jnp.einsum(
            "ihc,khc->hik", pieces[:, 0], pieces[:, 1], preferred_element_type=jnp.float32
        )
        scores = scores * (1.0 / math.sqrt(head_size)) + bias_key_last
        highest = jnp.max(scores, axis=-1, keepdims=True)
        exponent = jnp.exp(scores - highest)
        totals = jnp.sum(exponent, axis=-1)
        weights = exponent.astype(jnp.bfloat16)
        attended = jnp.einsum(
            "hik,khc->ihc", weights, pieces[:, 2], preferred_element_type=jnp.float32
        )
        attended = attended / jnp.swapaxes(totals, 0, 1)[..., None]
        gated_out = (attended * pieces[:, 3].astype(jnp.float32)).astype(jnp.bfloat16)
        return gated_out.reshape(width_n, heads_here * head_size)

    gated_cols = lax.map(attend, jnp.arange(row_count, dtype=jnp.int32))
    returned = lax.all_to_all(
        gated_cols.reshape(row_count, -1), "dap", split_axis=1, concat_axis=0, tiled=True
    )
    returned = returned.reshape(width_n, row_count, heads_here * head_size)
    update = lax.psum_scatter(
        jnp.einsum("jic,cd->ijd", returned, w_out, preferred_element_type=jnp.float32),
        "heads",
        scatter_dimension=0,
        tiled=True,
    )
    return update.astype(jnp.bfloat16)


def fits(mesh, pair, w_project, w_bias):
    n, groups = mesh.shape["dap"], mesh.shape["heads"]
    rows, width, channels = pair.shape
    devices = n * groups
    heads = w_bias.shape[1] * groups
    return (
        groups == 2
        and channels == 128
        and width <= 128
        and width % devices == 0
        and width % 32 == 0
        and w_project.shape[2] * groups == 128
        and n % 8 == 0
        and rows % groups == 0
    )


def solution(mesh):
    n, groups = mesh.shape["dap"], mesh.shape["heads"]

    def run(pair, ln_gain, ln_shift, w_project, w_bias, w_out):
        if fits(mesh, pair, w_project, w_bias):
            return fused(n, groups, pair, ln_gain, ln_shift, w_project, w_bias, w_out)
        return local(pair, ln_gain, ln_shift, w_project, w_bias, w_out)

    in_specs = (
        P("dap", None, None),
        P(),
        P(),
        P(None, None, "heads"),
        P(None, "heads"),
        P("heads", None),
    )
    out_specs = P(("dap", "heads"), None, None)
    return jax.shard_map(run, mesh=mesh, in_specs=in_specs, out_specs=out_specs, check_vma=False)
```

```python
import functools
import math

import jax
import jax.numpy as jnp
from jax import lax
from jax.experimental import pallas as pl
from jax.experimental.pallas import tpu as pltpu
from jax.sharding import PartitionSpec as P

MESH = pl.DeviceIdType.MESH
F32 = jnp.float32
BF16 = jnp.bfloat16
NT = (((1,), (1,)), ((), ()))
VMEM_BYTES = 60 * 1024 * 1024


def up(size, unit):
    return -(-size // unit) * unit


def nt_dot(left, right):
    return lax.dot_general(left, right, NT, preferred_element_type=F32)


def kernel(
    dims,
    pair_hbm,
    gain_hbm,
    shift_hbm,
    bias_hbm,
    project_hbm,
    w_out_hbm,
    out_ref,
    pair_ref,
    gain_ref,
    shift_ref,
    bias_ref,
    normed,
    stage,
    x_send,
    x_recv,
    tokens,
    w_all,
    b_pad,
    b_recv,
    bias,
    gated,
    g_stage,
    g_send,
    g_recv,
    projected,
    load_sem,
    w_send_sem,
    w_recv_sem,
    x_send_sem,
    x_recv_sem,
    b_send_sem,
    b_recv_sem,
    g_send_sem,
    g_recv_sem,
):
    n, groups, rows, width, cols, heads, size = dims
    own_heads = heads // groups
    inner = own_heads * size
    devices = n * groups
    own_rows = rows // groups
    d = lax.axis_index("dap")
    g = lax.axis_index("heads")
    me = g * n + d
    quad = min(4, n)
    slabs = n // quad
    z, r = d // quad, lax.rem(d, quad)
    planes = [g, 1 - g]
    dap_at = [lax.rem(d + offset, n) for offset in range(n)]
    slab_at = [lax.rem(z + back, slabs) * quad for back in range(slabs)]
    near_at = [lax.rem(r + near, quad) for near in range(quad)]

    low_out = 4 * inner
    loads = [
        pltpu.make_async_copy(pair_hbm, pair_ref, load_sem.at[0]),
        pltpu.make_async_copy(gain_hbm, gain_ref, load_sem.at[4]),
        pltpu.make_async_copy(shift_hbm, shift_ref, load_sem.at[5]),
    ]
    w_loads = [
        pltpu.make_async_copy(bias_hbm, bias_ref, load_sem.at[1]),
        pltpu.make_async_copy(project_hbm, w_all.at[g, pl.ds(0, low_out)], load_sem.at[2]),
        pltpu.make_async_copy(w_out_hbm, w_all.at[g, pl.ds(low_out, inner)], load_sem.at[3]),
    ]
    for copy in loads + w_loads:
        copy.start()

    barrier = pltpu.get_barrier_semaphore()
    others = [(k % n, k // n) for k in range(1, devices)]
    for offset, plane in others:
        pl.semaphore_signal(
            barrier, inc=1, device_id=(dap_at[offset], planes[plane]), device_id_type=MESH
        )

    for copy in loads:
        copy.wait()
    gain = gain_ref[...]
    shift = shift_ref[...]
    for a in range(rows):
        values = pair_ref[a].astype(F32)
        average = jnp.mean(values, axis=-1, keepdims=True)
        centred = values - average
        variance = jnp.mean(centred * centred, axis=-1, keepdims=True)
        normed[a * 128 : a * 128 + width, :] = (
            centred * lax.rsqrt(variance + 1e-05) * gain + shift
        )

    x_rows = x_send.shape[1]
    for a in range(rows):
        for c in range(cols):
            start = pl.multiple_of(a * 128 + c * devices + g * n, 8)
            stage[pl.ds(a * cols + c, n, x_rows), :] = normed[pl.ds(start, n), :]
    x_send[...] = stage[...].reshape(n, x_rows, -1).astype(BF16)

    w_loads[0].wait()
    b_pad[0:own_heads, :] = bias_ref[...]
    w_bias = b_pad[...]
    part = nt_dot(w_bias, normed[...].astype(BF16))
    for a in range(rows):
        for h in range(own_heads):
            row = h * rows + a
            b_recv[d, g, row : row + 1, :] = part[h : h + 1, a * 128 : (a + 1) * 128]
    for c in range(cols):
        tokens[c * 128 + width : (c + 1) * 128, :] = jnp.zeros((128 - width, 128), F32)
    for copy in w_loads[1:]:
        copy.wait()

    pl.semaphore_wait(barrier, devices - 1)

    def send(src, dst, send_sem, recv_sem, other, plane=g):
        copy = pltpu.make_async_remote_copy(
            src_ref=src,
            dst_ref=dst,
            send_sem=send_sem,
            recv_sem=recv_sem,
            device_id=(other, plane),
            device_id_type=MESH,
        )
        copy.start()
        return copy

    def drain(ref, sem):
        pltpu.make_async_copy(ref, ref, sem).wait()

    far = [near + back * quad for back in range(1, slabs) for near in range(quad)]
    for offset in far + list(range(1, quad)):
        other = slab_at[offset // quad] + near_at[offset % quad]
        send(x_send.at[other], x_recv.at[d], x_send_sem, x_recv_sem, other)

    b_used = own_heads * rows
    own_bias = b_recv.at[d, g, pl.ds(0, b_used)]
    first = [(back, plane) for plane in range(groups) for back in range(slabs)][1:]
    across = {}
    for back, plane in first:
        k = back * groups + plane
        across[back, plane] = send(
            own_bias, own_bias, b_send_sem.at[0], b_recv_sem.at[k], slab_at[back] + r, planes[plane]
        )

    own_w = w_all.at[g]
    w_copy = send(own_w, own_w, w_send_sem, w_recv_sem, d, planes[1])
    x_recv[d] = x_send[d]

    for back in range(slabs):
        for plane in range(groups):
            if back or plane:
                across[back, plane].wait_recv()
        block = slab_at[(slabs - back) % slabs] + r
        both = b_recv.at[block, :, pl.ds(0, b_used)]
        for near in range(1, quad):
            send(both, both, b_send_sem.at[1], b_recv_sem.at[0], slab_at[0] + near_at[near])

    drain(x_recv.at[pl.ds(0, n - 1)], x_recv_sem)
    stage[...] = x_recv[...].reshape(n * x_rows, -1).astype(F32)
    for a in range(rows):
        for c in range(cols):
            tokens[pl.ds(c * 128 + a, n, rows), :] = stage[pl.ds(a * cols + c, n, x_rows), :]
    entries = tokens[...].astype(BF16)

    w_copy.wait_recv()

    def weight(t):
        low = t * inner
        return jnp.concatenate([w_all[k, low : low + inner, :] for k in range(groups)], axis=0)

    keys = nt_dot(entries, weight(1)).astype(BF16)
    channels = heads * size
    w_rest = jnp.concatenate([weight(0), weight(2), weight(3)], axis=0)
    rest = nt_dot(w_rest, entries)
    queries = rest[:channels].astype(BF16)
    all_values = rest[channels : 2 * channels].astype(BF16)
    gating = jax.nn.sigmoid(rest[2 * channels :]).astype(BF16).astype(F32)
    lane = lax.broadcasted_iota(jnp.int32, (width, channels), 1) // size
    row = lax.broadcasted_iota(jnp.int32, (channels, 128), 0) // size
    scores, values = [], []
    for c in range(cols):
        key = keys[c * 128 : c * 128 + width]
        stacked = jnp.concatenate(
            [jnp.where(lane == h, key, jnp.zeros_like(key)) for h in range(heads)], axis=0
        )
        part = slice(c * 128, (c + 1) * 128)
        scores.append(jnp.dot(stacked, queries[:, part], preferred_element_type=F32))
        value = all_values[:, part]
        values.append(
            jnp.concatenate(
                [jnp.where(row == h, value, jnp.zeros_like(value)) for h in range(heads)], axis=1
            )
        )

    passed = slabs * (quad - 1)
    drain(b_recv.at[pl.ds(0, passed), :, pl.ds(0, b_used)], b_recv_sem.at[0])
    b_rows = b_recv.shape[2]
    gathered = b_recv.reshape(n * groups * b_rows, 128)
    for h in range(heads):
        for a in range(rows):
            first_row = h // own_heads * b_rows + h % own_heads * rows + a
            bias[pl.ds(h * width + a, n, rows), :] = gathered[
                pl.ds(first_row, n, groups * b_rows), :
            ]

    scale = 1.0 / math.sqrt(size)
    blank = jnp.zeros((128 - width, 128), BF16)
    for c in range(cols):
        weights, inverse = [], []
        for h in range(heads):
            part = slice(h * width, (h + 1) * width)
            score = scores[c][part] * scale + bias[part, :]
            exponent = jnp.exp(score - jnp.max(score, axis=0, keepdims=True))
            total = jnp.sum(exponent, axis=0, keepdims=True)
            weights += [exponent.astype(BF16), blank]
            inverse.append(jnp.broadcast_to(1.0 / total, (size, 128)))
        attended = jnp.dot(values[c], jnp.concatenate(weights, axis=0), preferred_element_type=F32)
        result = attended * jnp.concatenate(inverse, axis=0) * gating[:, c * 128 : (c + 1) * 128]
        gated[c * 128 : (c + 1) * 128, :] = result.T

    g_rows = g_send.shape[1]
    for i in range(own_rows):
        for c in range(cols):
            g_stage[pl.ds(i * cols + c, devices, g_rows), :] = gated[
                pl.ds(c * 128 + i, devices, own_rows), :
            ]
    g_send[...] = g_stage[...].reshape(devices, g_rows, -1).astype(BF16)

    for offset, plane in sorted(others, key=lambda o: -min(o[0], n - o[0])):
        other_d, other_g = dap_at[offset], planes[plane]
        send(
            g_send.at[other_d * groups + other_g],
            g_recv.at[me],
            g_send_sem,
            g_recv_sem,
            other_d,
            other_g,
        )
    g_recv[me] = g_send[d * groups + g]
    drain(b_recv.at[pl.ds(0, len(first)), 0, pl.ds(0, b_used)], b_send_sem.at[0])
    drain(b_recv.at[pl.ds(0, passed), :, pl.ds(0, b_used)], b_send_sem.at[1])
    drain(x_send.at[pl.ds(0, n - 1)], x_send_sem)
    w_copy.wait_send()
    drain(g_send.at[pl.ds(0, devices - 1)], g_send_sem)
    w_out = jnp.concatenate([w_all[k, low_out : low_out + inner, :] for k in range(groups)], axis=0)
    drain(g_recv.at[pl.ds(0, devices - 1)], g_recv_sem)
    projected[...] = jnp.dot(
        g_recv[...].reshape(devices * g_rows, -1), w_out, preferred_element_type=F32
    )
    for i in range(own_rows):
        for c in range(cols):
            out_ref[i, c * devices : (c + 1) * devices, :] = projected[
                pl.ds(i * cols + c, devices, g_rows), :
            ].astype(BF16)


def fused(n, groups, pair, ln_gain, ln_shift, w_project, w_bias, w_out):
    rows, width, channels = pair.shape
    own_heads = w_bias.shape[1]
    heads = own_heads * groups
    size = w_project.shape[2] // own_heads
    devices = n * groups
    cols = width // devices
    own_rows = rows // groups
    inner = own_heads * size
    w_rows = 5 * inner
    b_rows = up(own_heads * rows, 8)
    x_rows = up(rows * cols, 16)
    g_rows = up(own_rows * cols, 16)
    dims = (n, groups, rows, width, cols, heads, size)
    vmem = pl.BlockSpec(memory_space=pltpu.VMEM)
    hbm = pl.BlockSpec(memory_space=pl.ANY)
    sems = pltpu.SemaphoreType.DMA
    return pl.pallas_call(
        functools.partial(kernel, dims),
        out_shape=pltpu.VMEM((own_rows, width, channels), BF16),
        in_specs=[hbm] * 6,
        out_specs=vmem,
        scratch_shapes=[
            pltpu.VMEM((rows, width, channels), BF16),
            pltpu.VMEM((1, channels), F32),
            pltpu.VMEM((1, channels), F32),
            pltpu.VMEM((own_heads, channels), BF16),
            pltpu.VMEM((rows * 128, channels), F32),
            pltpu.VMEM((n * x_rows, channels), F32),
            pltpu.VMEM((n, x_rows, channels), BF16),
            pltpu.VMEM((n, x_rows, channels), BF16),
            pltpu.VMEM((cols * 128, channels), F32),
            pltpu.VMEM((groups, w_rows, channels), BF16),
            pltpu.VMEM((16, channels), BF16),
            pltpu.VMEM((n, groups, b_rows, 128), F32),
            pltpu.VMEM((heads * width, 128), F32),
            pltpu.VMEM((cols * 128, heads * size), F32),
            pltpu.VMEM((devices * g_rows, heads * size), F32),
            pltpu.VMEM((devices, g_rows, heads * size), BF16),
            pltpu.VMEM((devices, g_rows, heads * size), BF16),
            pltpu.VMEM((devices * g_rows, channels), F32),
            sems((6,)),
            sems(()),
            sems(()),
            sems(()),
            sems(()),
            sems((2,)),
            sems((n // min(4, n) * groups,)),
            sems(()),
            sems(()),
        ],
        compiler_params=pltpu.CompilerParams(
            collective_id=0, has_side_effects=True, vmem_limit_bytes=VMEM_BYTES
        ),
    )(
        pair,
        ln_gain.reshape(1, -1),
        ln_shift.reshape(1, -1),
        w_bias.T,
        jnp.transpose(w_project, (1, 2, 0)).reshape(-1, channels),
        w_out,
    )


def normalize(pair, ln_gain, ln_shift):
    values_f = pair.astype(jnp.float32)
    average = jnp.mean(values_f, axis=-1, keepdims=True)
    centred = values_f - average
    variance = jnp.mean(centred * centred, axis=-1, keepdims=True)
    return (centred * lax.rsqrt(variance + 1e-05) * ln_gain + ln_shift).astype(jnp.bfloat16)


def project_entries(normed, flat_w):
    projected = jnp.dot(normed, flat_w, preferred_element_type=jnp.float32)
    head_width = flat_w.shape[1] // 4
    head_part = projected[..., : 3 * head_width].astype(jnp.bfloat16)
    gating = jax.nn.sigmoid(projected[..., 3 * head_width :]).astype(jnp.bfloat16)
    return jnp.concatenate([head_part, gating], axis=-1)


def local(pair, ln_gain, ln_shift, w_project, w_bias, w_out):
    row_count, width_n, channels = pair.shape
    heads_here = w_bias.shape[1]
    head_size = w_project.shape[2] // heads_here
    flat_w = w_project.reshape(channels, -1)
    normed_rows = normalize(pair, ln_gain, ln_shift)
    bias_rows = jnp.einsum("abc,ch->hab", normed_rows, w_bias, preferred_element_type=jnp.float32)
    bias_all = lax.all_gather(bias_rows, "dap", axis=1, tiled=True)
    bias_key_last = jnp.swapaxes(bias_all, 1, 2)
    dap_count = lax.axis_size("dap")
    blocks = pair.reshape(row_count, dap_count, width_n // dap_count, channels)
    packed = project_entries(
        normalize(
            lax.all_to_all(blocks, "dap", split_axis=1, concat_axis=0, tiled=True),
            ln_gain,
            ln_shift,
        ),
        flat_w,
    )
    packed = packed.reshape(width_n, row_count, -1)

    def attend(index):
        column_data = lax.dynamic_index_in_dim(packed, index, 1, keepdims=False)
        pieces = column_data.reshape(width_n, 4, heads_here, head_size)
        scores = jnp.einsum(
            "ihc,khc->hik", pieces[:, 0], pieces[:, 1], preferred_element_type=jnp.float32
        )
        scores = scores * (1.0 / math.sqrt(head_size)) + bias_key_last
        highest = jnp.max(scores, axis=-1, keepdims=True)
        exponent = jnp.exp(scores - highest)
        totals = jnp.sum(exponent, axis=-1)
        weights = exponent.astype(jnp.bfloat16)
        attended = jnp.einsum(
            "hik,khc->ihc", weights, pieces[:, 2], preferred_element_type=jnp.float32
        )
        attended = attended / jnp.swapaxes(totals, 0, 1)[..., None]
        gated_out = (attended * pieces[:, 3].astype(jnp.float32)).astype(jnp.bfloat16)
        return gated_out.reshape(width_n, heads_here * head_size)

    gated_cols = lax.map(attend, jnp.arange(row_count, dtype=jnp.int32))
    returned = lax.all_to_all(
        gated_cols.reshape(row_count, -1), "dap", split_axis=1, concat_axis=0, tiled=True
    )
    returned = returned.reshape(width_n, row_count, heads_here * head_size)
    update = lax.psum_scatter(
        jnp.einsum("jic,cd->ijd", returned, w_out, preferred_element_type=jnp.float32),
        "heads",
        scatter_dimension=0,
        tiled=True,
    )
    return update.astype(jnp.bfloat16)


def fits(mesh, pair, w_project, w_bias):
    n, groups = mesh.shape["dap"], mesh.shape["heads"]
    rows, width, channels = pair.shape
    devices = n * groups
    heads = w_bias.shape[1] * groups
    return (
        groups == 2
        and channels == 128
        and width <= 128
        and width % devices == 0
        and width % 32 == 0
        and w_project.shape[2] * groups == 128
        and n % 8 == 0
        and rows % groups == 0
    )


def solution(mesh):
    n, groups = mesh.shape["dap"], mesh.shape["heads"]

    def run(pair, ln_gain, ln_shift, w_project, w_bias, w_out):
        if fits(mesh, pair, w_project, w_bias):
            return fused(n, groups, pair, ln_gain, ln_shift, w_project, w_bias, w_out)
        return local(pair, ln_gain, ln_shift, w_project, w_bias, w_out)

    in_specs = (
        P("dap", None, None),
        P(),
        P(),
        P(None, None, "heads"),
        P(None, "heads"),
        P("heads", None),
    )
    out_specs = P(("dap", "heads"), None, None)
    return jax.shard_map(run, mesh=mesh, in_specs=in_specs, out_specs=out_specs, check_vma=False)
```
